32 devices in a mesh: branch: 8 (over z, y), head: 4 (over x, core).
Axes of the slice: x: 2, y: 2, z: 4, core: 2. Of those that a mesh axis runs over, the one named last changes fastest.
Arguments:
- q_latent: bfloat16 [1024, 1536], P(('branch', 'head')), may hold values from -6 to 6
- seg_latent: bfloat16 [1024, 576], P(('branch', 'head')), may hold values from -6 to 6
- trunk_latent: bfloat16 [4096, 576], P(('branch', 'head'))
- visible: int32 [8, 4096], P('branch'), may hold values from 0 to 1, as said below
- w_uq: bfloat16 [1536, 24576], P(None, 'head'), may hold values from -0.15625 to 0.15625
- w_uk: bfloat16 [128, 128, 512], P('head'), may hold values from -0.25 to 0.25
- w_uv: bfloat16 [128, 512, 128], P('head'), may hold values from -0.25 to 0.25
Outputs:
- attended: bfloat16 [1024, 16384], P('branch', 'head')
The draws below stay inside these ranges and needn't reach their ends.
Inputs may be any that keep to these rules, and one draw needn't show every extreme that they name: `visible`: every branch sees the trunk rows 0 to 1023, then exactly one of four runs of consecutive rows that cover rows 1024 to 3071, and one of eight runs covering the last quarter; the run of the last quarter is one of two children of the branch's run of the middle half. Runs have random lengths and may be empty.
All inputs are finite; a program needn't handle non-finite values.
Results may differ from the reference program's by a relative error of at most 0.009.
The reference program's roundings to bfloat16 on the way count: a program that leaves them out, or rounds other values in their place, can miss the bound.
Values may be sent and summed in bfloat16 or wider, within the bound.
No kernel may reach another device: no remote copies, remote signals or barrier semaphores. Data moves between devices by JAX's collectives and lax.ppermute only.
A program may use at most 128 MiB of HBM per device.

```python
import jax
import jax.numpy as jnp
from jax import lax

H = 128
QR = 1536
KR = 512
RD = 64
ND = 128
VD = 128
SEG = 128
TRUNK = 4096
BRANCHES = 8


def draw_trunk_latent(key, part):
    key = jax.random.fold_in(key, 11)
    normal_key = jax.random.fold_in(key, 0)
    values = jax.random.normal(normal_key, (TRUNK, KR + RD), jnp.float32)
    return values.astype(jnp.bfloat16)


def draw_visible(key, part):
    key = jax.random.fold_in(key, 23)
    cut_key, second_key, node_key, child_key = jax.random.split(key, 4)
    quarter = TRUNK // 4
    cuts_mid = jnp.sort(jax.random.randint(cut_key, (3,), quarter, 3 * quarter + 1))
    cuts_end = jnp.sort(jax.random.randint(second_key, (7,), 3 * quarter, TRUNK + 1))
    rows = jnp.arange(TRUNK, dtype=jnp.int32)
    node_mid = jnp.sum((rows[:, None] >= cuts_mid[None, :]).astype(jnp.int32), axis=1)
    node_end = jnp.sum((rows[:, None] >= cuts_end[None, :]).astype(jnp.int32), axis=1)
    branch_mid = jax.random.randint(node_key, (BRANCHES,), 0, 4)
    branch_end = 2 * branch_mid + jax.random.randint(child_key, (BRANCHES,), 0, 2)
    root = rows[None, :] < quarter
    middle = (rows[None, :] >= quarter) & (rows[None, :] < 3 * quarter) & (node_mid[None, :] == branch_mid[:, None])
    last = (rows[None, :] >= 3 * quarter) & (node_end[None, :] == branch_end[:, None])
    return (root | middle | last).astype(jnp.int32)


def steps_of(own_key, dims, pieces, least, high):
    factor_of = 1.0
    for dim, blocks in pieces:
        steps = jax.random.uniform(jax.random.fold_in(jax.random.fold_in(own_key, 6), dim), (blocks,), jnp.float32, least / len(pieces), high / len(pieces))
        factor_of = factor_of * jnp.repeat(jnp.exp(steps), dims[dim] // blocks).reshape((-1,) + (1,) * (len(dims) - 1 - dim))
    return factor_of


def gaussian(rng, shape, scale, reach, cuts=(), kind=jnp.bfloat16):
    values = scale * jax.random.normal(rng, shape, jnp.float32)
    if cuts:
        values = values * steps_of(rng, shape, cuts, -0.22, 0.18)
    return jnp.clip(values, -reach, reach).astype(kind)


def setup_inputs(seed: int = 0) -> dict:
    key_of = jax.random.split(jax.random.key(seed), 8)
    q_latent = gaussian(key_of[0], (BRANCHES * SEG, QR), 1.0, 6.0, ((0, 32),))
    seg_latent = gaussian(key_of[1], (BRANCHES * SEG, KR + RD), 1.0, 6.0, ((0, 32),))
    trunk_latent = draw_trunk_latent(jax.random.fold_in(key_of[7], 71), 0)
    visible = draw_visible(jax.random.fold_in(key_of[7], 71), 0)
    w_uq = gaussian(key_of[4], (QR, H * (ND + RD)), QR ** -0.5, 0.15625, ((1, 4),))
    w_uk = gaussian(key_of[5], (H, ND, KR), KR ** -0.5, 0.25, ((0, 4),))
    w_uv = gaussian(key_of[6], (H, KR, VD), KR ** -0.5, 0.25, ((0, 4),))
    return dict(q_latent=q_latent, seg_latent=seg_latent, trunk_latent=trunk_latent, visible=visible, w_uq=w_uq, w_uk=w_uk, w_uv=w_uv)


def rotate(values, positions):
    half = values.shape[-1] // 2
    freq = 10000.0 ** (-2.0 * jnp.arange(half, dtype=jnp.float32) / values.shape[-1])
    angle = positions.astype(jnp.float32)[:, None, None] * freq[None, None, :]
    first = values[..., :half]
    second = values[..., half:]
    cosine = jnp.cos(angle)
    sine = jnp.sin(angle)
    return jnp.concatenate([first * cosine - second * sine, first * sine + second * cosine], axis=-1)


def reference(q_latent, seg_latent, trunk_latent, visible, w_uq, w_uk, w_uv):
    q_rows = q_latent.reshape(BRANCHES, SEG, QR)
    seg_rows = seg_latent.reshape(BRANCHES, SEG, KR + RD)
    scale = 1.0 / (ND + RD) ** 0.5
    causal = jnp.arange(SEG, dtype=jnp.int32)[None, :] <= jnp.arange(SEG, dtype=jnp.int32)[:, None]

    def one_branch(items):
        ql, sl, seen = items
        depth = jnp.sum(seen).astype(jnp.int32)
        positions = depth + jnp.arange(SEG, dtype=jnp.int32)
        q_full = jnp.dot(ql, w_uq, preferred_element_type=jnp.float32).reshape(SEG, H, ND + RD)
        q_nope = q_full[..., :ND].astype(jnp.bfloat16)
        q_rope = rotate(q_full[..., ND:], positions).astype(jnp.bfloat16)
        q_abs = jnp.einsum("shn,hnk->shk", q_nope.astype(jnp.float32), w_uk.astype(jnp.float32)).astype(jnp.bfloat16)
        query = jnp.concatenate([q_abs, q_rope], axis=-1)
        keys = jnp.concatenate([trunk_latent, sl], axis=0)
        allowed = jnp.concatenate([jnp.broadcast_to(seen[None, :] > 0, (SEG, TRUNK)), causal], axis=1)
        scores = jnp.einsum("shc,kc->shk", query.astype(jnp.float32), keys.astype(jnp.float32)) * scale
        scores = jnp.where(allowed[:, None, :], scores, -1e30)
        peak = jnp.max(scores, axis=-1, keepdims=True)
        weights = jnp.where(allowed[:, None, :], jnp.exp(scores - peak), 0.0)
        total = jnp.sum(weights, axis=-1)
        weights = weights.astype(jnp.bfloat16)
        summed = jnp.einsum("shk,kc->shc", weights.astype(jnp.float32), keys[:, :KR].astype(jnp.float32))
        attend = (summed / total[..., None]).astype(jnp.bfloat16)
        result = jnp.einsum("shc,hcv->shv", attend.astype(jnp.float32), w_uv.astype(jnp.float32))
        return result.astype(jnp.bfloat16).reshape(SEG, H * VD)

    return lax.map(one_branch, (q_rows, seg_rows, visible)).reshape(BRANCHES * SEG, H * VD)
```

```python
import functools

import jax
import jax.numpy as jnp
from jax import lax
from jax.experimental import pallas as pl
from jax.experimental.pallas import tpu as pltpu
from jax.sharding import PartitionSpec as P

AXES = ("branch", "head")
BLOCK = 128
HIDDEN = -1e30
LOG2E = 1.4426950408889634
NT = (((1,), (1,)), ((), ()))


def query_kernel(qs_ref, cos_ref, sin_ref, wuq_ref, wuk_ref, out_ref, *, rope):
    group, nope, lat = wuk_ref.shape
    width = nope + rope
    half = rope // 2
    q = jnp.dot(qs_ref[...], wuq_ref[...], preferred_element_type=jnp.float32)
    for g in range(group):
        q_nope = q[:, g * width : g * width + nope].astype(jnp.bfloat16)
        x = q[:, g * width + nope : (g + 1) * width]
        swapped = jnp.concatenate([x[:, half:], x[:, :half]], axis=1)
        q_rope = x * cos_ref[...] + swapped * sin_ref[...]
        q_abs = jnp.dot(q_nope, wuk_ref[g], preferred_element_type=jnp.float32)
        out_ref[g, :, :lat] = q_abs.astype(jnp.bfloat16)
        out_ref[g, :, lat:] = q_rope.astype(jnp.bfloat16)


def make_query(qs, cosine, sine, w_uq, w_uk, group=8):
    seg_len = qs.shape[0]
    rank = w_uq.shape[0]
    heads, nope, lat = w_uk.shape
    width = w_uq.shape[1] // heads
    rope = width - nope
    group = min(group, heads)
    return pl.pallas_call(
        functools.partial(query_kernel, rope=rope),
        grid=(heads // group,),
        in_specs=[
            pl.BlockSpec((seg_len, rank), lambda i: (0, 0)),
            pl.BlockSpec((seg_len, rope), lambda i: (0, 0)),
            pl.BlockSpec((seg_len, rope), lambda i: (0, 0)),
            pl.BlockSpec((rank, group * width), lambda i: (0, i)),
            pl.BlockSpec((group, nope, lat), lambda i: (i, 0, 0)),
        ],
        out_specs=pl.BlockSpec((group, seg_len, lat + rope), lambda i: (i, 0, 0)),
        out_shape=jax.ShapeDtypeStruct((heads, seg_len, lat + rope), jnp.bfloat16),
        compiler_params=pltpu.CompilerParams(vmem_limit_bytes=32 << 20),
        cost_estimate=pl.CostEstimate(
            flops=2 * seg_len * heads * (rank * width + nope * lat),
            bytes_accessed=2 * (w_uq.size + w_uk.size + seg_len * heads * (lat + rope)),
            transcendentals=0,
        ),
        name="query",
    )(qs, cosine, sine, w_uq, w_uk)


def lane_sums(p):
    return functools.reduce(
        jnp.add, [p[:, j : j + 128] for j in range(0, p.shape[1], 128)]
    )


def attend_kernel(
    counts, owners, q_ref, seg_ref, seen_ref, wuv_ref, *rest, pieces, sub, wide, scale
):
    piece_refs, out_ref = rest[:pieces], rest[pieces]
    keys, bias, m_ref, l_ref, acc_ref, meta, sem = rest[pieces + 1 :]
    group, lat, vd = wuv_ref.shape
    s = seg_ref.shape[1]
    blocks = counts.shape[0]
    root = blocks // 4
    factor = scale * LOG2E

    @pl.when(pl.program_id(0) == 0)
    def _():
        def place(i, at):
            meta[i] = at
            return at + (counts[i] > 0).astype(jnp.int32)

        used = lax.fori_loop(0, blocks, place, jnp.int32(1))
        meta[blocks] = used

        def moves(act):
            k = 0
            for ref in piece_refs:
                for j in range(ref.shape[0]):
                    def move(owner, source, ref=ref, j=j):
                        @pl.when(counts[owner] > 0)
                        def _():
                            lane = pl.multiple_of(meta[owner] * BLOCK, BLOCK)
                            act(
                                pltpu.make_async_copy(
                                    source, keys.at[:, pl.ds(lane, BLOCK)], sem
                                )
                            )

                    for t in range(ref.shape[2] // BLOCK):
                        move(owners[k], ref.at[j, :, pl.ds(t * BLOCK, BLOCK)])
                        k += 1

        moves(lambda copy: copy.start())
        keys[:, :BLOCK] = seg_ref[...]
        bias[:, :BLOCK] = jnp.zeros((1, BLOCK), jnp.float32)

        def fill(i, carry):
            @pl.when(counts[i] > 0)
            def _():
                mark = seen_ref[:, pl.ds(pl.multiple_of(i * BLOCK, BLOCK), BLOCK)]
                lane = pl.multiple_of(meta[i] * BLOCK, BLOCK)
                bias[:, pl.ds(lane, BLOCK)] = jnp.where(mark > 0, 0.0, HIDDEN)

            return carry

        lax.fori_loop(0, blocks, fill, 0)
        moves(lambda copy: copy.wait())

    used = meta[blocks]
    per = sub // s
    subs = group // per

    def rows(k):
        return pl.ds(k * sub, sub)

    def query(k):
        return q_ref[k * per : (k + 1) * per].reshape(sub, q_ref.shape[2])

    first = (1 + root) * BLOCK
    k0 = keys[:, :first]
    v0 = keys[:lat, :first]
    row = lax.broadcasted_iota(jnp.int32, (s, first), 0)
    col = lax.broadcasted_iota(jnp.int32, (s, first), 1)
    own = jnp.where((col <= row) | (col >= s), bias[:, :first], HIDDEN)
    for k in range(subs):
        raw = jnp.dot(query(k), k0, preferred_element_type=jnp.float32)
        sc = (raw.reshape(per, s, first) + own[None]).reshape(sub, first)
        m = jnp.max(sc, axis=1, keepdims=True)
        p = jnp.exp2((sc - m) * factor)
        m_ref[rows(k), :] = jnp.broadcast_to(m, (sub, 128))
        l_ref[rows(k), :] = lane_sums(p)
        acc_ref[rows(k), :] = lax.dot_general(
            p.astype(jnp.bfloat16), v0, NT, preferred_element_type=jnp.float32
        )

    def chunk(lane, size):
        lane = pl.multiple_of(lane, BLOCK)
        kk = keys[:, pl.ds(lane, size)]
        vv = keys[:lat, pl.ds(lane, size)]
        hide = bias[:, pl.ds(lane, size)]
        for k in range(subs):
            sc = jnp.dot(query(k), kk, preferred_element_type=jnp.float32) + hide
            old = m_ref[rows(k), :]
            m = jnp.maximum(old, jnp.max(sc, axis=1, keepdims=True))
            fade = jnp.exp2((old - m) * factor)
            p = jnp.exp2((sc - jnp.tile(m, (1, size // 128))) * factor)
            m_ref[rows(k), :] = m
            l_ref[rows(k), :] = l_ref[rows(k), :] * fade + lane_sums(p)
            acc_ref[rows(k), :] = acc_ref[rows(k), :] * jnp.tile(
                fade, (1, lat // 128)
            ) + lax.dot_general(
                p.astype(jnp.bfloat16), vv, NT, preferred_element_type=jnp.float32
            )

    left = used - (1 + root)
    many = left // wide

    def big(i, carry):
        chunk(first + i * (wide * BLOCK), wide * BLOCK)
        return carry

    lax.fori_loop(0, many, big, 0)
    at = first + many * (wide * BLOCK)
    rem = left - many * wide
    size = wide // 2
    while size:
        take = rem >= size

        @pl.when(take)
        def _(at=at, size=size):
            chunk(at, size * BLOCK)

        at = at + jnp.where(take, size * BLOCK, 0)
        rem = rem - jnp.where(take, size, 0)
        size //= 2

    for g in range(group):
        r = pl.ds(g * s, s)
        total = jnp.sum(l_ref[r, :], axis=1, keepdims=True)
        o = (acc_ref[r, :] * (1.0 / total)).astype(jnp.bfloat16)
        out_ref[:, g * vd : (g + 1) * vd] = jnp.dot(
            o, wuv_ref[g], preferred_element_type=jnp.float32
        ).astype(jnp.bfloat16)


def attend(counts, owners, query, seg_t, seen, w_uv, pieces, scale, group=8, sub=1024, wide=4):
    heads, s, depth = query.shape
    lat, vd = w_uv.shape[1:]
    trunk = seen.shape[1]
    group = min(group, heads)
    sub = min(sub, group * s)
    total = group * s
    return pl.pallas_call(
        functools.partial(
            attend_kernel, pieces=len(pieces), sub=sub, wide=wide, scale=scale
        ),
        grid_spec=pltpu.PrefetchScalarGridSpec(
            num_scalar_prefetch=2,
            grid=(heads // group,),
            in_specs=[
                pl.BlockSpec((group, s, depth), lambda i, *_: (i, 0, 0)),
                pl.BlockSpec((depth, s), lambda i, *_: (0, 0)),
                pl.BlockSpec((1, trunk), lambda i, *_: (0, 0)),
                pl.BlockSpec((group, lat, vd), lambda i, *_: (i, 0, 0)),
            ]
            + [pl.BlockSpec(memory_space=pl.ANY)] * len(pieces),
            out_specs=pl.BlockSpec((s, group * vd), lambda i, *_: (0, i)),
            scratch_shapes=[
                pltpu.VMEM((depth, trunk + BLOCK), jnp.bfloat16),
                pltpu.VMEM((1, trunk + BLOCK), jnp.float32),
                pltpu.VMEM((total, 128), jnp.float32),
                pltpu.VMEM((total, 128), jnp.float32),
                pltpu.VMEM((total, lat), jnp.float32),
                pltpu.SMEM((trunk // BLOCK + 1,), jnp.int32),
                pltpu.SemaphoreType.DMA,
            ],
        ),
        out_shape=jax.ShapeDtypeStruct((s, heads * vd), jnp.bfloat16),
        compiler_params=pltpu.CompilerParams(vmem_limit_bytes=56 << 20),
        cost_estimate=pl.CostEstimate(
            flops=2 * heads * s * (trunk // 2) * (depth + lat),
            bytes_accessed=2 * (query.size + w_uv.size + trunk * depth),
            transcendentals=heads * s * trunk // 2,
        ),
        name="attend",
    )(counts, owners, query, seg_t, seen, w_uv, *pieces)


def gather_trunk(trunk, branches, heads):
    devices = branches * heads
    me = lax.axis_index("branch") * heads + lax.axis_index("head")
    if trunk.shape[0] != BLOCK or branches != 8 or heads != 4:
        whole = lax.all_gather(trunk, AXES, axis=0, tiled=True)
        return [whole.T[None]], jnp.arange(whole.shape[0] // BLOCK, dtype=jnp.int32)

    def send(x, by_core):
        pairs = [(i, i ^ by_core[i & 1]) for i in range(devices)]
        return lax.ppermute(x, AXES, pairs)

    mine = trunk.T[None]
    column = jnp.concatenate([mine] + [send(mine, (8 * d, 8 * d)) for d in (1, 2, 3)], axis=0)
    side = send(column, (2, 4))
    both = jnp.concatenate([column, side], axis=0)
    cross = send(both, (4, 2))
    here = [both, cross]
    there = [send(both, (1, 1)), send(cross, (1, 1))]
    core = me & 1
    one, two = 2 + 2 * core, 4 - 2 * core
    steps = jnp.arange(4, dtype=jnp.int32) * 8
    mine_of = lambda one, two: jnp.concatenate(
        [steps, steps ^ one, steps ^ two, steps ^ one ^ two]
    )
    owners = jnp.concatenate([me ^ mine_of(one, two), me ^ 1 ^ mine_of(two, one)])
    return here + there, owners


def make_shards(branches, heads):
    def shards(q_latent, seg_latent, trunk_latent, visible, w_uq, w_uk, w_uv):
        heads_here, nope, lat = w_uk.shape
        rope = w_uq.shape[1] // heads_here - nope
        half = rope // 2
        scale = 1.0 / (nope + rope) ** 0.5
        rank = q_latent.shape[1]
        joined = lax.all_gather(
            jnp.concatenate([q_latent, seg_latent], axis=1), "head", axis=0, tiled=True
        )
        pieces, owners = gather_trunk(trunk_latent, branches, heads)
        seg_len = joined.shape[0]
        counts = jnp.sum(visible.reshape(-1, BLOCK), axis=1)
        position = (jnp.sum(visible) + jnp.arange(seg_len, dtype=jnp.int32)).astype(jnp.float32)
        freq = 10000.0 ** (-2.0 * jnp.arange(half, dtype=jnp.float32) / rope)
        angle = position[:, None] * freq[None, :]
        cosine = jnp.cos(angle)
        sine = jnp.sin(angle)
        query = make_query(
            joined,
            jnp.concatenate([cosine, cosine], axis=1),
            jnp.concatenate([-sine, sine], axis=1),
            w_uq,
            w_uk,
        )
        return attend(
            counts, owners, query, joined[:, rank:].T, visible, w_uv, pieces, scale
        )

    return shards


def solution(mesh):
    placed = (
        P(("branch", "head"), None),
        P(("branch", "head"), None),
        P(("branch", "head"), None),
        P("branch", None),
        P(None, "head"),
        P("head", None, None),
        P("head", None, None),
    )
    return jax.shard_map(
        make_shards(mesh.shape["branch"], mesh.shape["head"]),
        mesh=mesh,
        in_specs=placed,
        out_specs=P("branch", "head"),
        check_vma=False,
    )
```

```python
import functools

import jax
import jax.numpy as jnp
import numpy as np
from jax import lax
from jax.experimental import pallas as pl
from jax.experimental.pallas import tpu as pltpu
from jax.sharding import PartitionSpec as P

AXES = ("branch", "head")
BLOCK = 128
HIDDEN = -1e30
LOG2E = 1.4426950408889634
NT = (((1,), (1,)), ((), ()))


def staged(count, score, absorb):
    ahead = score(0)
    for k in range(count):
        now = ahead
        if k + 1 < count:
            ahead = score(k + 1)
        absorb(k, now)


def owner_of(me, spot):
    offset, mask, plane = spot
    if mask is None:
        return jnp.int32(offset)
    return offset + (lax.rem(me, jnp.int32(plane)) ^ mask)


def query_kernel(me, *refs, pieces, spots, aliased):
    piece_refs = refs[:pieces]
    seen_ref, freq_ref, wuq_ref, wuk_ref = refs[pieces : pieces + 4]
    out_ref, qs, cos_ref, sin_ref = refs[pieces + 4 + aliased :]
    group, nope, lat = wuk_ref.shape
    rope = freq_ref.shape[1]
    width = nope + rope
    half = rope // 2

    @pl.when(pl.program_id(0) == 0)
    def _():
        for ref, spot in zip(piece_refs, spots):
            n = ref.shape[0]
            at = owner_of(me[0], spot)
            qs[pl.ds(pl.multiple_of(at * n, n), n), :] = ref[...]
        depth = jnp.sum(seen_ref[...].astype(jnp.float32), axis=1, keepdims=True)
        token = lax.broadcasted_iota(jnp.int32, cos_ref.shape, 0).astype(jnp.float32)
        angle = (token + depth) * freq_ref[...]
        side = lax.broadcasted_iota(jnp.int32, cos_ref.shape, 1)
        sine = jnp.sin(angle)
        cos_ref[...] = jnp.cos(angle)
        sin_ref[...] = jnp.where(side < half, -sine, sine)

    def project(k):
        return jnp.dot(
            qs[...],
            wuq_ref[:, 2 * k * width : 2 * (k + 1) * width],
            preferred_element_type=jnp.float32,
        )

    def absorb(k, q):
        for j in range(2):
            g = 2 * k + j
            q_nope = q[:, j * width : j * width + nope].astype(jnp.bfloat16)
            x = q[:, j * width + nope : (j + 1) * width]
            swapped = jnp.concatenate([x[:, half:], x[:, :half]], axis=1)
            q_rope = x * cos_ref[...] + swapped * sin_ref[...]
            q_abs = jnp.dot(q_nope, wuk_ref[g], preferred_element_type=jnp.float32)
            out_ref[g, :, :lat] = q_abs.astype(jnp.bfloat16)
            out_ref[g, :, lat:] = q_rope.astype(jnp.bfloat16)

    staged(group // 2, project, absorb)


def make_query(me, pieces, spots, seen, w_uq, w_uk, start, count, before=None, group=8):
    seg_len = pieces[0].shape[0] * len(pieces)
    rank = w_uq.shape[0]
    heads, nope, lat = w_uk.shape
    width = w_uq.shape[1] // heads
    rope = width - nope
    group = min(group, count)
    base = start // group
    powers = 10000.0 ** (-2.0 * np.arange(rope // 2) / rope)
    freq = np.concatenate([powers, powers])[None].astype(np.float32)
    aliased = 0 if before is None else 1
    return pl.pallas_call(
        functools.partial(query_kernel, pieces=len(pieces), spots=spots, aliased=aliased),
        grid_spec=pltpu.PrefetchScalarGridSpec(
            num_scalar_prefetch=1,
            grid=(count // group,),
            in_specs=[pl.BlockSpec((p.shape[0], rank), lambda i, *_: (0, 0)) for p in pieces]
            + [
                pl.BlockSpec(seen.shape, lambda i, *_: (0, 0)),
                pl.BlockSpec(freq.shape, lambda i, *_: (0, 0)),
                pl.BlockSpec((rank, group * width), lambda i, *_: (0, base + i)),
                pl.BlockSpec((group, nope, lat), lambda i, *_: (base + i, 0, 0)),
            ]
            + [pl.BlockSpec(memory_space=pl.ANY)] * aliased,
            out_specs=pl.BlockSpec((group, seg_len, lat + rope), lambda i, *_: (base + i, 0, 0)),
            scratch_shapes=[
                pltpu.VMEM((seg_len, rank), jnp.bfloat16),
                pltpu.VMEM((seg_len, rope), jnp.float32),
                pltpu.VMEM((seg_len, rope), jnp.float32),
            ],
        ),
        out_shape=jax.ShapeDtypeStruct((heads, seg_len, lat + rope), jnp.bfloat16),
        input_output_aliases={len(pieces) + 5: 0} if aliased else {},
        compiler_params=pltpu.CompilerParams(vmem_limit_bytes=60 << 20),
        cost_estimate=pl.CostEstimate(
            flops=2 * seg_len * count * (rank * width + nope * lat),
            bytes_accessed=2 * count * (rank * width + nope * lat + seg_len * (lat + rope)),
            transcendentals=0,
        ),
        name="query",
    )(me, *pieces, seen, freq, w_uq, w_uk, *([before] if aliased else []))


def lane_sums(p):
    return functools.reduce(
        jnp.add, [p[:, j : j + 128] for j in range(0, p.shape[1], 128)]
    )


def root_kernel(
    me, q_ref, *rest, rows_n, pieces, row_spots, spots, sub, scale, lat
):
    row_refs, piece_refs = rest[:rows_n], rest[rows_n : rows_n + pieces]
    acc_ref, m_ref, l_ref, keys, own, sem = rest[rows_n + pieces :]
    s, depth = own.shape
    first = keys.shape[1]
    factor = scale * LOG2E

    @pl.when(pl.program_id(0) == 0)
    def _():
        copies = []
        for ref in piece_refs:
            for j in range(ref.shape[0]):
                for t in range(ref.shape[2] // BLOCK):
                    lane = pl.multiple_of((1 + owner_of(me[0], spots[len(copies)])) * BLOCK, BLOCK)
                    copies.append(
                        pltpu.make_async_copy(
                            ref.at[j, :, pl.ds(t * BLOCK, BLOCK)],
                            keys.at[:, pl.ds(lane, BLOCK)],
                            sem,
                        )
                    )
        for copy in copies:
            copy.start()
        for k, ref in enumerate(row_refs):
            n = ref.shape[0]
            at = owner_of(me[0], row_spots[k])
            own[pl.ds(pl.multiple_of(at * n, n), n), :] = ref[...]
        keys[:, :s] = own[...].T
        for copy in copies:
            copy.wait()

    per = sub // s
    row = lax.broadcasted_iota(jnp.int32, (s, s), 0)
    col = lax.broadcasted_iota(jnp.int32, (s, s), 1)
    causal = jnp.where(col <= row, 0.0, HIDDEN)

    def score(k):
        q = q_ref[k * per : (k + 1) * per].reshape(sub, depth)
        return jnp.dot(q, keys[...], preferred_element_type=jnp.float32)

    def absorb(k, raw):
        r = pl.ds(k * sub, sub)
        head = (raw[:, :s].reshape(per, s, s) + causal[None]).reshape(sub, s)
        sc = jnp.concatenate([head, raw[:, s:]], axis=1)
        m = jnp.max(sc, axis=1, keepdims=True)
        p = jnp.exp2((sc - m) * factor)
        m_ref[r, :] = jnp.broadcast_to(m, (sub, 128))
        l_ref[r, :] = lane_sums(p)
        acc_ref[r, :] = lax.dot_general(
            p.astype(jnp.bfloat16), keys[:lat, :], NT, preferred_element_type=jnp.float32
        )

    staged(q_ref.shape[0] // per, score, absorb)


def attend_root(me, row_spots, spots, query, row_pieces, pieces, root, lat, scale, group=8, sub=512):
    heads, s, depth = query.shape
    group = min(group, heads)
    sub = min(sub, group * s)
    total = group * s
    width = row_pieces[0].shape[1]
    out = lambda n: jax.ShapeDtypeStruct((heads * s, n), jnp.float32)
    return pl.pallas_call(
        functools.partial(
            root_kernel,
            rows_n=len(row_pieces),
            pieces=len(pieces),
            row_spots=row_spots,
            spots=spots,
            sub=sub,
            scale=scale,
            lat=lat,
        ),
        grid_spec=pltpu.PrefetchScalarGridSpec(
            num_scalar_prefetch=1,
            grid=(heads // group,),
            in_specs=[pl.BlockSpec((group, s, depth), lambda i, *_: (i, 0, 0))]
            + [pl.BlockSpec((p.shape[0], width), lambda i, *_: (0, 0)) for p in row_pieces]
            + [pl.BlockSpec(memory_space=pl.ANY)] * len(pieces),
            out_specs=[
                pl.BlockSpec((total, lat), lambda i, *_: (i, 0)),
                pl.BlockSpec((total, 128), lambda i, *_: (i, 0)),
                pl.BlockSpec((total, 128), lambda i, *_: (i, 0)),
            ],
            scratch_shapes=[
                pltpu.VMEM((depth, s + root), jnp.bfloat16),
                pltpu.VMEM((s, depth), jnp.bfloat16),
                pltpu.SemaphoreType.DMA,
            ],
        ),
        out_shape=[out(lat), out(128), out(128)],
        compiler_params=pltpu.CompilerParams(vmem_limit_bytes=60 << 20),
        cost_estimate=pl.CostEstimate(
            flops=4 * heads * s * (s + root) * (depth + lat),
            bytes_accessed=2 * query.size + 4 * heads * s * (lat + 256),
            transcendentals=heads * s * (s + root),
        ),
        name="attend_root",
    )(me, query, *row_pieces, *pieces)


def rest_kernel(
    counts, me, q_ref, acc_in, m_in, l_in, seen_ref, wuv_ref, *rest, pieces, spots, sub, wide, scale
):
    piece_refs, out_ref = rest[:pieces], rest[pieces]
    keys, bias, m_ref, l_ref, acc_ref, meta, sem = rest[pieces + 1 :]
    group, lat, vd = wuv_ref.shape
    s, depth = q_ref.shape[1:]
    blocks = counts.shape[0]
    root = blocks // 4
    factor = scale * LOG2E

    @pl.when(pl.program_id(0) == 0)
    def _():
        def place(i, at):
            meta[i] = at
            return at + (counts[i] > 0).astype(jnp.int32)

        used = lax.fori_loop(root, blocks, place, jnp.int32(0))
        meta[blocks] = used

        def moves(act):
            k = 0
            for ref in piece_refs:
                for j in range(ref.shape[0]):
                    for t in range(ref.shape[2] // BLOCK):
                        owner = owner_of(me[0], spots[k])
                        k += 1

                        @pl.when(counts[owner] > 0)
                        def _(owner=owner, ref=ref, j=j, t=t):
                            lane = pl.multiple_of(meta[owner] * BLOCK, BLOCK)
                            act(
                                pltpu.make_async_copy(
                                    ref.at[j, :, pl.ds(t * BLOCK, BLOCK)],
                                    keys.at[:, pl.ds(lane, BLOCK)],
                                    sem,
                                )
                            )

        moves(lambda copy: copy.start())

        def fill(i, carry):
            @pl.when(counts[i] > 0)
            def _():
                mark = seen_ref[:, pl.ds(pl.multiple_of(i * BLOCK, BLOCK), BLOCK)]
                lane = pl.multiple_of(meta[i] * BLOCK, BLOCK)
                bias[:, pl.ds(lane, BLOCK)] = jnp.where(mark > 0, 0.0, HIDDEN)

            return carry

        lax.fori_loop(root, blocks, fill, 0)
        lane = pl.multiple_of(used * BLOCK, BLOCK)
        keys[:, pl.ds(lane, BLOCK)] = jnp.zeros((depth, BLOCK), jnp.bfloat16)
        bias[:, pl.ds(lane, BLOCK)] = jnp.full((1, BLOCK), HIDDEN, jnp.float32)
        moves(lambda copy: copy.wait())

    used = meta[blocks]
    per = sub // s
    subs = group // per
    m_ref[...] = m_in[...]
    l_ref[...] = l_in[...]
    acc_ref[...] = acc_in[...]

    def chunk(lane, size):
        lane = pl.multiple_of(lane, BLOCK)
        hide = bias[:, pl.ds(lane, size)]

        def score(k):
            q = q_ref[k * per : (k + 1) * per].reshape(sub, depth)
            return jnp.dot(q, keys[:, pl.ds(lane, size)], preferred_element_type=jnp.float32)

        def absorb(k, raw):
            r = pl.ds(k * sub, sub)
            sc = raw + hide
            old = m_ref[r, :]
            m = jnp.maximum(old, jnp.max(sc, axis=1, keepdims=True))
            fade = jnp.exp2((old - m) * factor)
            p = jnp.exp2((sc - jnp.tile(m, (1, size // 128))) * factor)
            m_ref[r, :] = m
            l_ref[r, :] = l_ref[r, :] * fade + lane_sums(p)
            acc_ref[r, :] = acc_ref[r, :] * jnp.tile(fade, (1, lat // 128)) + lax.dot_general(
                p.astype(jnp.bfloat16),
                keys[:lat, pl.ds(lane, size)],
                NT,
                preferred_element_type=jnp.float32,
            )

        staged(subs, score, absorb)

    many = (used + 1) // wide

    def big(i, carry):
        chunk(i * (wide * BLOCK), wide * BLOCK)
        return carry

    lax.fori_loop(0, many, big, 0)

    @pl.when(used > many * wide)
    def _():
        chunk(many * (wide * BLOCK), wide // 2 * BLOCK)

    for g in range(group):
        r = pl.ds(g * s, s)
        total = jnp.sum(l_ref[r, :], axis=1, keepdims=True)
        o = (acc_ref[r, :] * (1.0 / total)).astype(jnp.bfloat16)
        out_ref[:, g * vd : (g + 1) * vd] = jnp.dot(
            o, wuv_ref[g], preferred_element_type=jnp.float32
        ).astype(jnp.bfloat16)


def attend_rest(counts, me, spots, query, state, seen, w_uv, pieces, scale, group=8, sub=1024, wide=4):
    heads, s, depth = query.shape
    lat, vd = w_uv.shape[1:]
    trunk = seen.shape[1]
    group = min(group, heads)
    sub = min(sub, group * s)
    total = group * s
    return pl.pallas_call(
        functools.partial(
            rest_kernel, pieces=len(pieces), spots=spots, sub=sub, wide=wide, scale=scale
        ),
        grid_spec=pltpu.PrefetchScalarGridSpec(
            num_scalar_prefetch=2,
            grid=(heads // group,),
            in_specs=[
                pl.BlockSpec((group, s, depth), lambda i, *_: (i, 0, 0)),
                pl.BlockSpec((total, lat), lambda i, *_: (i, 0)),
                pl.BlockSpec((total, 128), lambda i, *_: (i, 0)),
                pl.BlockSpec((total, 128), lambda i, *_: (i, 0)),
                pl.BlockSpec((1, trunk), lambda i, *_: (0, 0)),
                pl.BlockSpec((group, lat, vd), lambda i, *_: (i, 0, 0)),
            ]
            + [pl.BlockSpec(memory_space=pl.ANY)] * len(pieces),
            out_specs=pl.BlockSpec((s, group * vd), lambda i, *_: (0, i)),
            scratch_shapes=[
                pltpu.VMEM((depth, trunk), jnp.bfloat16),
                pltpu.VMEM((1, trunk), jnp.float32),
                pltpu.VMEM((total, 128), jnp.float32),
                pltpu.VMEM((total, 128), jnp.float32),
                pltpu.VMEM((total, lat), jnp.float32),
                pltpu.SMEM((trunk // BLOCK + 1,), jnp.int32),
                pltpu.SemaphoreType.DMA,
            ],
        ),
        out_shape=jax.ShapeDtypeStruct((s, heads * vd), jnp.bfloat16),
        compiler_params=pltpu.CompilerParams(vmem_limit_bytes=60 << 20),
        cost_estimate=pl.CostEstimate(
            flops=heads * s * (trunk // 2) * (depth + lat),
            bytes_accessed=2 * (query.size + w_uv.size) + 4 * heads * s * (lat + 256),
            transcendentals=heads * s * trunk // 4,
        ),
        name="attend_rest",
    )(counts, me, query, *state, seen, w_uv, *pieces)


def swap(x, mask, devices):
    return lax.ppermute(x, AXES, [(i, i ^ mask) for i in range(devices)])


def gather_rows(rows, branches, heads):
    devices = branches * heads
    if rows.shape[0] % 16 or heads & (heads - 1):
        return [lax.all_gather(rows, "head", axis=0, tiled=True)], [(0, None, 1)]
    pieces = [rows] + [swap(rows, k, devices) for k in range(1, heads)]
    return pieces, [(0, k, heads) for k in range(heads)]


def is_cube(trunk, branches, heads):
    return trunk.shape[0] == BLOCK and branches == 8 and heads == 4


def gather_columns(trunk, branches, heads):
    devices = branches * heads
    plane = devices // 4
    mine = trunk.T[None]
    column = [mine] + [swap(mine, plane * d, devices) for d in (1, 2, 3)]
    layer = (lax.axis_index("branch") * heads + lax.axis_index("head")) // plane
    level = jnp.concatenate(column, axis=0)
    return jnp.concatenate(
        [lax.dynamic_slice_in_dim(level, layer ^ k, 1, 0) for k in range(4)], axis=0
    )


def make_shards(branches, heads):
    devices = branches * heads
    plane = devices // 4

    def shards(q_latent, seg_latent, trunk_latent, visible, w_uq, w_uk, w_uv):
        heads_here, nope, lat = w_uk.shape
        rope = w_uq.shape[1] // heads_here - nope
        scale = 1.0 / (nope + rope) ** 0.5
        cube = is_cube(trunk_latent, branches, heads)
        place = (lax.axis_index("branch") * heads + lax.axis_index("head")).astype(jnp.int32)
        me = place.reshape(1)
        rows, row_spots = gather_rows(q_latent, branches, heads)
        counts = jnp.sum(visible.reshape(-1, BLOCK), axis=1)
        part = heads_here // 2
        project = functools.partial(make_query, me, rows, row_spots, visible, w_uq, w_uk)
        if cube:
            levels = gather_columns(trunk_latent, branches, heads)
            query = project(0, part)
            query, levels, seg_latent, counts = lax.optimization_barrier(
                (query, levels, seg_latent, counts)
            )
            root, others = levels[:1], levels[1:]
            around = (0, 2, 4, 6)
            root_here = [root] + [swap(root, k, devices) for k in around[1:]]
            query = project(part, heads_here - part, query)
            own, own_spots = gather_rows(seg_latent, branches, heads)
            query, root_here, others, own = lax.optimization_barrier(
                (query, root_here, others, own)
            )
            root_here = jnp.concatenate(root_here, axis=0)
            pieces = [root_here, swap(root_here, 1, devices)]
            masks = list(around) + [1 ^ k for k in around]
            root_spots = [(0, k, plane) for k in masks]
            rest = [others] + [swap(others, k, devices) for k in around[1:]]
            rest_spots = [(plane * d, k, plane) for k in masks for d in (1, 2, 3)]
        else:
            query = project(0, heads_here)
            own, own_spots = gather_rows(seg_latent, branches, heads)
            whole = lax.all_gather(trunk_latent, AXES, axis=0, tiled=True).T[None]
            size = whole.shape[2] // 4
            pieces, rest = [whole[:, :, :size]], [whole[:, :, size:]]
            spots = [(k, None, 1) for k in range(whole.shape[2] // BLOCK)]
            root_spots, rest_spots = spots[: size // BLOCK], spots[size // BLOCK :]
        state = attend_root(
            me, own_spots, root_spots, query, own, pieces, visible.shape[1] // 4, lat, scale
        )
        state, rest = lax.optimization_barrier((state, rest))
        if cube:
            rest = rest + [swap(x, 1, devices) for x in rest]
        return attend_rest(counts, me, rest_spots, query, state, visible, w_uv, rest, scale)

    return shards


def solution(mesh):
    placed = (
        P(("branch", "head"), None),
        P(("branch", "head"), None),
        P(("branch", "head"), None),
        P("branch", None),
        P(None, "head"),
        P("head", None, None),
        P("head", None, None),
    )
    return jax.shard_map(
        make_shards(mesh.shape["branch"], mesh.shape["head"]),
        mesh=mesh,
        in_specs=placed,
        out_specs=P("branch", "head"),
        check_vma=False,
    )
```

```python
import functools

import jax
import jax.numpy as jnp
import numpy as np
from jax import lax
from jax.experimental import pallas as pl
from jax.experimental.pallas import tpu as pltpu
from jax.sharding import PartitionSpec as P

AXES = ("branch", "head")
BLOCK = 128
HIDDEN = -1e30
LOG2E = 1.4426950408889634
NT = (((1,), (1,)), ((), ()))


def staged(count, score, absorb):
    ahead = score(0)
    for k in range(count):
        now = ahead
        if k + 1 < count:
            ahead = score(k + 1)
        absorb(k, now)


def owner_of(me, spot):
    offset, mask, plane = spot
    if mask is None:
        return jnp.int32(offset)
    return offset + (lax.rem(me, jnp.int32(plane)) ^ mask)


def query_kernel(me, *refs, pieces, spots, aliased):
    piece_refs = refs[:pieces]
    seen_ref, freq_ref, wuq_ref, wuk_ref = refs[pieces : pieces + 4]
    out_ref, qs, cos_ref, sin_ref = refs[pieces + 4 + aliased :]
    group, nope, lat = wuk_ref.shape
    rope = freq_ref.shape[1]
    width = nope + rope
    half = rope // 2

    @pl.when(pl.program_id(0) == 0)
    def _():
        for ref, spot in zip(piece_refs, spots):
            n = ref.shape[0]
            at = owner_of(me[0], spot)
            qs[pl.ds(pl.multiple_of(at * n, n), n), :] = ref[...]
        depth = jnp.sum(seen_ref[...].astype(jnp.float32), axis=1, keepdims=True)
        token = lax.broadcasted_iota(jnp.int32, cos_ref.shape, 0).astype(jnp.float32)
        angle = (token + depth) * freq_ref[...]
        side = lax.broadcasted_iota(jnp.int32, cos_ref.shape, 1)
        sine = jnp.sin(angle)
        cos_ref[...] = jnp.cos(angle)
        sin_ref[...] = jnp.where(side < half, -sine, sine)

    def project(k):
        return jnp.dot(
            qs[...],
            wuq_ref[:, 2 * k * width : 2 * (k + 1) * width],
            preferred_element_type=jnp.float32,
        )

    def absorb(k, q):
        for j in range(2):
            g = 2 * k + j
            q_nope = q[:, j * width : j * width + nope].astype(jnp.bfloat16)
            x = q[:, j * width + nope : (j + 1) * width]
            swapped = jnp.concatenate([x[:, half:], x[:, :half]], axis=1)
            q_rope = x * cos_ref[...] + swapped * sin_ref[...]
            q_abs = jnp.dot(q_nope, wuk_ref[g], preferred_element_type=jnp.float32)
            out_ref[g, :, :lat] = q_abs.astype(jnp.bfloat16)
            out_ref[g, :, lat:] = q_rope.astype(jnp.bfloat16)

    staged(group // 2, project, absorb)


def make_query(me, pieces, spots, seen, w_uq, w_uk, start, count, before=None, group=8):
    seg_len = pieces[0].shape[0] * len(pieces)
    rank = w_uq.shape[0]
    heads, nope, lat = w_uk.shape
    width = w_uq.shape[1] // heads
    rope = width - nope
    group = min(group, count)
    base = start // group
    powers = 10000.0 ** (-2.0 * np.arange(rope // 2) / rope)
    freq = np.concatenate([powers, powers])[None].astype(np.float32)
    aliased = 0 if before is None else 1
    return pl.pallas_call(
        functools.partial(query_kernel, pieces=len(pieces), spots=spots, aliased=aliased),
        grid_spec=pltpu.PrefetchScalarGridSpec(
            num_scalar_prefetch=1,
            grid=(count // group,),
            in_specs=[pl.BlockSpec((p.shape[0], rank), lambda i, *_: (0, 0)) for p in pieces]
            + [
                pl.BlockSpec(seen.shape, lambda i, *_: (0, 0)),
                pl.BlockSpec(freq.shape, lambda i, *_: (0, 0)),
                pl.BlockSpec((rank, group * width), lambda i, *_: (0, base + i)),
                pl.BlockSpec((group, nope, lat), lambda i, *_: (base + i, 0, 0)),
            ]
            + [pl.BlockSpec(memory_space=pl.ANY)] * aliased,
            out_specs=pl.BlockSpec((group, seg_len, lat + rope), lambda i, *_: (base + i, 0, 0)),
            scratch_shapes=[
                pltpu.VMEM((seg_len, rank), jnp.bfloat16),
                pltpu.VMEM((seg_len, rope), jnp.float32),
                pltpu.VMEM((seg_len, rope), jnp.float32),
            ],
        ),
        out_shape=jax.ShapeDtypeStruct((heads, seg_len, lat + rope), jnp.bfloat16),
        input_output_aliases={len(pieces) + 5: 0} if aliased else {},
        compiler_params=pltpu.CompilerParams(vmem_limit_bytes=60 << 20),
        cost_estimate=pl.CostEstimate(
            flops=2 * seg_len * count * (rank * width + nope * lat),
            bytes_accessed=2 * count * (rank * width + nope * lat + seg_len * (lat + rope)),
            transcendentals=0,
        ),
        name="query",
    )(me, *pieces, seen, freq, w_uq, w_uk, *([before] if aliased else []))


def lane_sums(p):
    return functools.reduce(
        jnp.add, [p[:, j : j + 128] for j in range(0, p.shape[1], 128)]
    )


def root_kernel(
    me, q_ref, *rest, rows_n, pieces, row_spots, spots, sub, scale, lat
):
    row_refs, piece_refs = rest[:rows_n], rest[rows_n : rows_n + pieces]
    acc_ref, m_ref, l_ref, keys, own, sem = rest[rows_n + pieces :]
    s, depth = own.shape
    first = keys.shape[1]
    factor = scale * LOG2E

    @pl.when(pl.program_id(0) == 0)
    def _():
        copies = []
        for ref in piece_refs:
            for j in range(ref.shape[0]):
                for t in range(ref.shape[2] // BLOCK):
                    lane = pl.multiple_of((1 + owner_of(me[0], spots[len(copies)])) * BLOCK, BLOCK)
                    copies.append(
                        pltpu.make_async_copy(
                            ref.at[j, :, pl.ds(t * BLOCK, BLOCK)],
                            keys.at[:, pl.ds(lane, BLOCK)],
                            sem,
                        )
                    )
        for copy in copies:
            copy.start()
        for k, ref in enumerate(row_refs):
            n = ref.shape[0]
            at = owner_of(me[0], row_spots[k])
            own[pl.ds(pl.multiple_of(at * n, n), n), :] = ref[...]
        keys[:, :s] = own[...].T
        for copy in copies:
            copy.wait()

    per = sub // s
    row = lax.broadcasted_iota(jnp.int32, (s, s), 0)
    col = lax.broadcasted_iota(jnp.int32, (s, s), 1)
    causal = jnp.where(col <= row, 0.0, HIDDEN)

    def score(k):
        q = q_ref[k * per : (k + 1) * per].reshape(sub, depth)
        return jnp.dot(q, keys[...], preferred_element_type=jnp.float32)

    def absorb(k, raw):
        r = pl.ds(k * sub, sub)
        head = (raw[:, :s].reshape(per, s, s) + causal[None]).reshape(sub, s)
        sc = jnp.concatenate([head, raw[:, s:]], axis=1)
        m = jnp.max(sc, axis=1, keepdims=True)
        p = jnp.exp2((sc - m) * factor)
        m_ref[r, :] = jnp.broadcast_to(m, (sub, 128))
        l_ref[r, :] = lane_sums(p)
        acc_ref[r, :] = lax.dot_general(
            p.astype(jnp.bfloat16), keys[:lat, :], NT, preferred_element_type=jnp.float32
        )

    staged(q_ref.shape[0] // per, score, absorb)


def attend_root(me, row_spots, spots, query, row_pieces, pieces, root, lat, scale, group=8, sub=512):
    heads, s, depth = query.shape
    group = min(group, heads)
    sub = min(sub, group * s)
    total = group * s
    width = row_pieces[0].shape[1]
    out = lambda n: jax.ShapeDtypeStruct((heads * s, n), jnp.float32)
    return pl.pallas_call(
        functools.partial(
            root_kernel,
            rows_n=len(row_pieces),
            pieces=len(pieces),
            row_spots=row_spots,
            spots=spots,
            sub=sub,
            scale=scale,
            lat=lat,
        ),
        grid_spec=pltpu.PrefetchScalarGridSpec(
            num_scalar_prefetch=1,
            grid=(heads // group,),
            in_specs=[pl.BlockSpec((group, s, depth), lambda i, *_: (i, 0, 0))]
            + [pl.BlockSpec((p.shape[0], width), lambda i, *_: (0, 0)) for p in row_pieces]
            + [pl.BlockSpec(memory_space=pl.ANY)] * len(pieces),
            out_specs=[
                pl.BlockSpec((total, lat), lambda i, *_: (i, 0)),
                pl.BlockSpec((total, 128), lambda i, *_: (i, 0)),
                pl.BlockSpec((total, 128), lambda i, *_: (i, 0)),
            ],
            scratch_shapes=[
                pltpu.VMEM((depth, s + root), jnp.bfloat16),
                pltpu.VMEM((s, depth), jnp.bfloat16),
                pltpu.SemaphoreType.DMA,
            ],
        ),
        out_shape=[out(lat), out(128), out(128)],
        compiler_params=pltpu.CompilerParams(vmem_limit_bytes=60 << 20),
        cost_estimate=pl.CostEstimate(
            flops=4 * heads * s * (s + root) * (depth + lat),
            bytes_accessed=2 * query.size + 4 * heads * s * (lat + 256),
            transcendentals=heads * s * (s + root),
        ),
        name="attend_root",
    )(me, query, *row_pieces, *pieces)


def rest_kernel(
    spans, me, q_ref, acc_in, m_in, l_in, wuv_ref, *rest, pieces, spots, sub, wide, scale
):
    piece_refs, out_ref = rest[:pieces], rest[pieces]
    raw, keys, m_ref, l_ref, acc_ref, meta, sem = rest[pieces + 1 :]
    group, lat, vd = wuv_ref.shape
    s, depth = q_ref.shape[1:]
    blocks = spans.shape[1]
    root = blocks // 4
    factor = scale * LOG2E

    @pl.when(pl.program_id(0) == 0)
    def _():
        def place(i, at):
            meta[i] = at
            return at + (spans[0, i] > 0).astype(jnp.int32)

        lax.fori_loop(root, blocks, place, jnp.int32(0))

        def moves(act):
            k = 0
            for ref in piece_refs:
                for j in range(ref.shape[0]):
                    for t in range(ref.shape[2] // BLOCK):
                        owner = owner_of(me[0], spots[k])
                        k += 1

                        @pl.when(spans[0, owner] > 0)
                        def _(owner=owner, ref=ref, j=j, t=t):
                            lane = pl.multiple_of(meta[owner] * BLOCK, BLOCK)
                            act(
                                pltpu.make_async_copy(
                                    ref.at[j, :, pl.ds(t * BLOCK, BLOCK)],
                                    raw.at[:, pl.ds(lane, BLOCK)],
                                    sem,
                                )
                            )

        moves(lambda copy: copy.start())
        moves(lambda copy: copy.wait())
        spot = lax.broadcasted_iota(jnp.int32, (depth, BLOCK), 1)

        def pack(i, total):
            @pl.when(spans[0, i] > 0)
            def _():
                offset = total & (BLOCK - 1)
                turn = (total + BLOCK - spans[1, i]) & (BLOCK - 1)
                block = raw[:, pl.ds(pl.multiple_of(meta[i] * BLOCK, BLOCK), BLOCK)]
                block = pltpu.roll(block.astype(jnp.float32), turn, 1)
                lane = pl.multiple_of(total - offset, BLOCK)
                here = keys[:, pl.ds(lane, BLOCK)].astype(jnp.float32)
                here = jnp.where(spot >= offset, block, here)
                keys[:, pl.ds(lane, BLOCK)] = here.astype(jnp.bfloat16)
                keys[:, pl.ds(lane + BLOCK, BLOCK)] = block.astype(jnp.bfloat16)

            return total + spans[0, i]

        total = lax.fori_loop(root, blocks, pack, jnp.int32(0))
        meta[blocks] = total
        lane = pl.multiple_of((total + BLOCK - 1) & -BLOCK, BLOCK)
        keys[:, pl.ds(lane, BLOCK)] = jnp.zeros((depth, BLOCK), jnp.bfloat16)

    seen = meta[blocks]
    used = lax.div(seen + (BLOCK - 1), jnp.int32(BLOCK))
    per = sub // s
    subs = group // per
    m_ref[...] = m_in[...]
    l_ref[...] = l_in[...]
    acc_ref[...] = acc_in[...]

    def chunk(lane, size):
        lane = pl.multiple_of(lane, BLOCK)
        index = lane + lax.broadcasted_iota(jnp.int32, (1, size), 1)
        hide = jnp.where(index < seen, 0.0, HIDDEN)

        def score(k):
            q = q_ref[k * per : (k + 1) * per].reshape(sub, depth)
            return jnp.dot(q, keys[:, pl.ds(lane, size)], preferred_element_type=jnp.float32)

        def absorb(k, raw):
            r = pl.ds(k * sub, sub)
            sc = raw + hide
            old = m_ref[r, :]
            m = jnp.maximum(old, jnp.max(sc, axis=1, keepdims=True))
            fade = jnp.exp2((old - m) * factor)
            p = jnp.exp2((sc - jnp.tile(m, (1, size // 128))) * factor)
            m_ref[r, :] = m
            l_ref[r, :] = l_ref[r, :] * fade + lane_sums(p)
            acc_ref[r, :] = acc_ref[r, :] * jnp.tile(fade, (1, lat // 128)) + lax.dot_general(
                p.astype(jnp.bfloat16),
                keys[:lat, pl.ds(lane, size)],
                NT,
                preferred_element_type=jnp.float32,
            )

        staged(subs, score, absorb)

    many = (used + 1) // wide

    def big(i, carry):
        chunk(i * (wide * BLOCK), wide * BLOCK)
        return carry

    lax.fori_loop(0, many, big, 0)

    @pl.when(used > many * wide)
    def _():
        chunk(many * (wide * BLOCK), wide // 2 * BLOCK)

    for g in range(group):
        r = pl.ds(g * s, s)
        total = jnp.sum(l_ref[r, :], axis=1, keepdims=True)
        o = (acc_ref[r, :] * (1.0 / total)).astype(jnp.bfloat16)
        out_ref[:, g * vd : (g + 1) * vd] = jnp.dot(
            o, wuv_ref[g], preferred_element_type=jnp.float32
        ).astype(jnp.bfloat16)


def attend_rest(spans, me, spots, query, state, w_uv, pieces, scale, group=8, sub=1024, wide=4):
    heads, s, depth = query.shape
    lat, vd = w_uv.shape[1:]
    trunk = spans.shape[1] * BLOCK
    group = min(group, heads)
    sub = min(sub, group * s)
    total = group * s
    return pl.pallas_call(
        functools.partial(
            rest_kernel, pieces=len(pieces), spots=spots, sub=sub, wide=wide, scale=scale
        ),
        grid_spec=pltpu.PrefetchScalarGridSpec(
            num_scalar_prefetch=2,
            grid=(heads // group,),
            in_specs=[
                pl.BlockSpec((group, s, depth), lambda i, *_: (i, 0, 0)),
                pl.BlockSpec((total, lat), lambda i, *_: (i, 0)),
                pl.BlockSpec((total, 128), lambda i, *_: (i, 0)),
                pl.BlockSpec((total, 128), lambda i, *_: (i, 0)),
                pl.BlockSpec((group, lat, vd), lambda i, *_: (i, 0, 0)),
            ]
            + [pl.BlockSpec(memory_space=pl.ANY)] * len(pieces),
            out_specs=pl.BlockSpec((s, group * vd), lambda i, *_: (0, i)),
            scratch_shapes=[
                pltpu.VMEM((depth, trunk), jnp.bfloat16),
                pltpu.VMEM((depth, trunk), jnp.bfloat16),
                pltpu.VMEM((total, 128), jnp.float32),
                pltpu.VMEM((total, 128), jnp.float32),
                pltpu.VMEM((total, lat), jnp.float32),
                pltpu.SMEM((trunk // BLOCK + 1,), jnp.int32),
                pltpu.SemaphoreType.DMA,
            ],
        ),
        out_shape=jax.ShapeDtypeStruct((s, heads * vd), jnp.bfloat16),
        compiler_params=pltpu.CompilerParams(vmem_limit_bytes=60 << 20),
        cost_estimate=pl.CostEstimate(
            flops=heads * s * (trunk // 2) * (depth + lat),
            bytes_accessed=2 * (query.size + w_uv.size) + 4 * heads * s * (lat + 256),
            transcendentals=heads * s * trunk // 4,
        ),
        name="attend_rest",
    )(spans, me, query, *state, w_uv, *pieces)


def swap(x, mask, devices):
    return lax.ppermute(x, AXES, [(i, i ^ mask) for i in range(devices)])


def gather_rows(rows, branches, heads):
    devices = branches * heads
    if rows.shape[0] % 16 or heads & (heads - 1):
        return [lax.all_gather(rows, "head", axis=0, tiled=True)], [(0, None, 1)]
    pieces = [rows] + [swap(rows, k, devices) for k in range(1, heads)]
    return pieces, [(0, k, heads) for k in range(heads)]


def is_cube(trunk, branches, heads):
    return trunk.shape[0] == BLOCK and branches == 8 and heads == 4


def gather_columns(trunk, branches, heads):
    devices = branches * heads
    plane = devices // 4
    mine = trunk.T[None]
    column = [mine] + [swap(mine, plane * d, devices) for d in (1, 2, 3)]
    layer = (lax.axis_index("branch") * heads + lax.axis_index("head")) // plane
    level = jnp.concatenate(column, axis=0)
    return jnp.concatenate(
        [lax.dynamic_slice_in_dim(level, layer ^ k, 1, 0) for k in range(4)], axis=0
    )


def block_spans(visible):
    marks = visible.reshape(-1, BLOCK)
    spot = jnp.arange(BLOCK, dtype=jnp.int32)[None, :]
    first = jnp.min(jnp.where(marks > 0, spot, BLOCK), axis=1)
    return jnp.stack([jnp.sum(marks, axis=1), first])


def make_shards(branches, heads):
    devices = branches * heads
    plane = devices // 4

    def shards(q_latent, seg_latent, trunk_latent, visible, w_uq, w_uk, w_uv):
        heads_here, nope, lat = w_uk.shape
        rope = w_uq.shape[1] // heads_here - nope
        scale = 1.0 / (nope + rope) ** 0.5
        cube = is_cube(trunk_latent, branches, heads)
        place = (lax.axis_index("branch") * heads + lax.axis_index("head")).astype(jnp.int32)
        me = place.reshape(1)
        rows, row_spots = gather_rows(q_latent, branches, heads)
        part = heads_here // 2
        project = functools.partial(make_query, me, rows, row_spots, visible, w_uq, w_uk)
        if cube:
            levels = gather_columns(trunk_latent, branches, heads)
            query = project(0, part)
            query, marks = lax.optimization_barrier((query, visible))
            spans = block_spans(marks)
            query, levels, seg_latent, spans = lax.optimization_barrier(
                (query, levels, seg_latent, spans)
            )
            root, others = levels[:1], levels[1:]
            around = (0, 2, 4, 6)
            root_here = [root] + [swap(root, k, devices) for k in around[1:]]
            query = project(part, heads_here - part, query)
            own, own_spots = gather_rows(seg_latent, branches, heads)
            query, root_here, others, own = lax.optimization_barrier(
                (query, root_here, others, own)
            )
            root_here = jnp.concatenate(root_here, axis=0)
            pieces = [root_here, swap(root_here, 1, devices)]
            masks = list(around) + [1 ^ k for k in around]
            root_spots = [(0, k, plane) for k in masks]
            rest = [others] + [swap(others, k, devices) for k in around[1:]]
            rest_spots = [(plane * d, k, plane) for k in masks for d in (1, 2, 3)]
        else:
            query = project(0, heads_here)
            spans = block_spans(visible)
            own, own_spots = gather_rows(seg_latent, branches, heads)
            whole = lax.all_gather(trunk_latent, AXES, axis=0, tiled=True).T[None]
            size = whole.shape[2] // 4
            pieces, rest = [whole[:, :, :size]], [whole[:, :, size:]]
            spots = [(k, None, 1) for k in range(whole.shape[2] // BLOCK)]
            root_spots, rest_spots = spots[: size // BLOCK], spots[size // BLOCK :]
        state = attend_root(
            me, own_spots, root_spots, query, own, pieces, visible.shape[1] // 4, lat, scale
        )
        state, rest = lax.optimization_barrier((state, rest))
        if cube:
            rest = rest + [swap(x, 1, devices) for x in rest]
        return attend_rest(spans, me, rest_spots, query, state, w_uv, rest, scale)

    return shards


def solution(mesh):
    placed = (
        P(("branch", "head"), None),
        P(("branch", "head"), None),
        P(("branch", "head"), None),
        P("branch", None),
        P(None, "head"),
        P("head", None, None),
        P("head", None, None),
    )
    return jax.shard_map(
        make_shards(mesh.shape["branch"], mesh.shape["head"]),
        mesh=mesh,
        in_specs=placed,
        out_specs=P("branch", "head"),
        check_vma=False,
    )
```

```python
import functools

import jax
import jax.numpy as jnp
import numpy as np
from jax import lax
from jax.experimental import pallas as pl
from jax.experimental.pallas import tpu as pltpu
from jax.sharding import PartitionSpec as P

AXES = ("branch", "head")
BLOCK = 128
HIDDEN = -1e30
LOG2E = 1.4426950408889634
NT = (((1,), (1,)), ((), ()))


def staged(count, score, absorb):
    ahead = score(0)
    for k in range(count):
        now = ahead
        if k + 1 < count:
            ahead = score(k + 1)
        absorb(k, now)


def in_hbm(x):
    return pltpu.with_memory_space_constraint(x, pltpu.HBM)


def owner_of(me, spot):
    offset, mask, plane = spot
    if mask is None:
        return jnp.int32(offset)
    return offset + (lax.rem(me, jnp.int32(plane)) ^ mask)


def query_kernel(me, *refs, pieces, spots, aliased):
    piece_refs = refs[:pieces]
    seen_ref, freq_ref, wuq_ref, wuk_ref = refs[pieces : pieces + 4]
    out_ref, qs, cos_ref, sin_ref = refs[pieces + 4 + aliased :]
    group, nope, lat = wuk_ref.shape
    rope = freq_ref.shape[1]
    width = nope + rope
    half = rope // 2

    @pl.when(pl.program_id(0) == 0)
    def _():
        for ref, spot in zip(piece_refs, spots):
            n = ref.shape[0]
            at = owner_of(me[0], spot)
            qs[pl.ds(pl.multiple_of(at * n, n), n), :] = ref[...]
        depth = jnp.sum(seen_ref[...].astype(jnp.float32), axis=1, keepdims=True)
        token = lax.broadcasted_iota(jnp.int32, cos_ref.shape, 0).astype(jnp.float32)
        angle = (token + depth) * freq_ref[...]
        side = lax.broadcasted_iota(jnp.int32, cos_ref.shape, 1)
        sine = jnp.sin(angle)
        cos_ref[...] = jnp.cos(angle)
        sin_ref[...] = jnp.where(side < half, -sine, sine)

    def project(k):
        return jnp.dot(
            qs[...],
            wuq_ref[:, 2 * k * width : 2 * (k + 1) * width],
            preferred_element_type=jnp.float32,
        )

    def absorb(k, q):
        for j in range(2):
            g = 2 * k + j
            q_nope = q[:, j * width : j * width + nope].astype(jnp.bfloat16)
            x = q[:, j * width + nope : (j + 1) * width]
            swapped = jnp.concatenate([x[:, half:], x[:, :half]], axis=1)
            q_rope = x * cos_ref[...] + swapped * sin_ref[...]
            q_abs = jnp.dot(q_nope, wuk_ref[g], preferred_element_type=jnp.float32)
            out_ref[g, :, :lat] = q_abs.astype(jnp.bfloat16)
            out_ref[g, :, lat:] = q_rope.astype(jnp.bfloat16)

    staged(group // 2, project, absorb)


def make_query(me, pieces, spots, seen, w_uq, w_uk, start, count, before=None, group=8):
    seg_len = pieces[0].shape[0] * len(pieces)
    rank = w_uq.shape[0]
    heads, nope, lat = w_uk.shape
    width = w_uq.shape[1] // heads
    rope = width - nope
    group = min(group, count)
    base = start // group
    powers = 10000.0 ** (-2.0 * np.arange(rope // 2) / rope)
    freq = np.concatenate([powers, powers])[None].astype(np.float32)
    aliased = 0 if before is None else 1
    return pl.pallas_call(
        functools.partial(query_kernel, pieces=len(pieces), spots=spots, aliased=aliased),
        grid_spec=pltpu.PrefetchScalarGridSpec(
            num_scalar_prefetch=1,
            grid=(count // group,),
            in_specs=[pl.BlockSpec((p.shape[0], rank), lambda i, *_: (0, 0)) for p in pieces]
            + [
                pl.BlockSpec(seen.shape, lambda i, *_: (0, 0)),
                pl.BlockSpec(freq.shape, lambda i, *_: (0, 0)),
                pl.BlockSpec((rank, group * width), lambda i, *_: (0, base + i)),
                pl.BlockSpec((group, nope, lat), lambda i, *_: (base + i, 0, 0)),
            ]
            + [pl.BlockSpec(memory_space=pl.ANY)] * aliased,
            out_specs=pl.BlockSpec((group, seg_len, lat + rope), lambda i, *_: (base + i, 0, 0)),
            scratch_shapes=[
                pltpu.VMEM((seg_len, rank), jnp.bfloat16),
                pltpu.VMEM((seg_len, rope), jnp.float32),
                pltpu.VMEM((seg_len, rope), jnp.float32),
            ],
        ),
        out_shape=jax.ShapeDtypeStruct((heads, seg_len, lat + rope), jnp.bfloat16),
        input_output_aliases={len(pieces) + 5: 0} if aliased else {},
        compiler_params=pltpu.CompilerParams(vmem_limit_bytes=60 << 20),
        cost_estimate=pl.CostEstimate(
            flops=2 * seg_len * count * (rank * width + nope * lat),
            bytes_accessed=2 * count * (rank * width + nope * lat + seg_len * (lat + rope)),
            transcendentals=0,
        ),
        name="query",
    )(me, *pieces, seen, freq, w_uq, w_uk, *([before] if aliased else []))


def lane_sums(p):
    return functools.reduce(
        jnp.add, [p[:, j : j + 128] for j in range(0, p.shape[1], 128)]
    )


def root_kernel(
    me, q_ref, *rest, rows_n, pieces, row_spots, spots, sub, scale, lat
):
    row_refs, piece_refs = rest[:rows_n], rest[rows_n : rows_n + pieces]
    acc_ref, m_ref, l_ref, keys, own, sem = rest[rows_n + pieces :]
    s, depth = own.shape
    first = keys.shape[1]
    factor = scale * LOG2E

    @pl.when(pl.program_id(0) == 0)
    def _():
        copies = []
        for ref in piece_refs:
            for j in range(ref.shape[0]):
                for t in range(ref.shape[2] // BLOCK):
                    lane = pl.multiple_of((1 + owner_of(me[0], spots[len(copies)])) * BLOCK, BLOCK)
                    copies.append(
                        pltpu.make_async_copy(
                            ref.at[j, :, pl.ds(t * BLOCK, BLOCK)],
                            keys.at[:, pl.ds(lane, BLOCK)],
                            sem,
                        )
                    )
        for copy in copies:
            copy.start()
        for k, ref in enumerate(row_refs):
            n = ref.shape[0]
            at = owner_of(me[0], row_spots[k])
            own[pl.ds(pl.multiple_of(at * n, n), n), :] = ref[...]
        keys[:, :s] = own[...].T
        for copy in copies:
            copy.wait()

    per = sub // s
    row = lax.broadcasted_iota(jnp.int32, (s, s), 0)
    col = lax.broadcasted_iota(jnp.int32, (s, s), 1)
    causal = jnp.where(col <= row, 0.0, HIDDEN)

    def score(k):
        q = q_ref[k * per : (k + 1) * per].reshape(sub, depth)
        return jnp.dot(q, keys[...], preferred_element_type=jnp.float32)

    def absorb(k, raw):
        r = pl.ds(k * sub, sub)
        head = (raw[:, :s].reshape(per, s, s) + causal[None]).reshape(sub, s)
        sc = jnp.concatenate([head, raw[:, s:]], axis=1)
        m = jnp.max(sc, axis=1, keepdims=True)
        p = jnp.exp2((sc - m) * factor)
        m_ref[r, :] = jnp.broadcast_to(m, (sub, 128))
        l_ref[r, :] = lane_sums(p)
        acc_ref[r, :] = lax.dot_general(
            p.astype(jnp.bfloat16), keys[:lat, :], NT, preferred_element_type=jnp.float32
        )

    staged(q_ref.shape[0] // per, score, absorb)


def attend_root(me, row_spots, spots, query, row_pieces, pieces, root, lat, scale, group=8, sub=512):
    heads, s, depth = query.shape
    group = min(group, heads)
    sub = min(sub, group * s)
    total = group * s
    width = row_pieces[0].shape[1]
    out = lambda n: jax.ShapeDtypeStruct((heads * s, n), jnp.float32)
    return pl.pallas_call(
        functools.partial(
            root_kernel,
            rows_n=len(row_pieces),
            pieces=len(pieces),
            row_spots=row_spots,
            spots=spots,
            sub=sub,
            scale=scale,
            lat=lat,
        ),
        grid_spec=pltpu.PrefetchScalarGridSpec(
            num_scalar_prefetch=1,
            grid=(heads // group,),
            in_specs=[pl.BlockSpec((group, s, depth), lambda i, *_: (i, 0, 0))]
            + [pl.BlockSpec((p.shape[0], width), lambda i, *_: (0, 0)) for p in row_pieces]
            + [pl.BlockSpec(memory_space=pl.ANY)] * len(pieces),
            out_specs=[
                pl.BlockSpec((total, lat), lambda i, *_: (i, 0)),
                pl.BlockSpec((total, 128), lambda i, *_: (i, 0)),
                pl.BlockSpec((total, 128), lambda i, *_: (i, 0)),
            ],
            scratch_shapes=[
                pltpu.VMEM((depth, s + root), jnp.bfloat16),
                pltpu.VMEM((s, depth), jnp.bfloat16),
                pltpu.SemaphoreType.DMA,
            ],
        ),
        out_shape=[out(lat), out(128), out(128)],
        compiler_params=pltpu.CompilerParams(vmem_limit_bytes=60 << 20),
        cost_estimate=pl.CostEstimate(
            flops=4 * heads * s * (s + root) * (depth + lat),
            bytes_accessed=2 * query.size + 4 * heads * s * (lat + 256),
            transcendentals=heads * s * (s + root),
        ),
        name="attend_root",
    )(me, in_hbm(query), *map(in_hbm, row_pieces), *map(in_hbm, pieces))


def rest_kernel(
    spans, me, q_ref, acc_in, m_in, l_in, wuv_ref, *rest, pieces, spots, sub, wide, scale
):
    piece_refs, out_ref = rest[:pieces], rest[pieces]
    raw, keys, m_ref, l_ref, acc_ref, meta, sem = rest[pieces + 1 :]
    group, lat, vd = wuv_ref.shape
    s, depth = q_ref.shape[1:]
    blocks = spans.shape[1]
    root = blocks // 4
    factor = scale * LOG2E

    @pl.when(pl.program_id(0) == 0)
    def _():
        def place(i, at):
            meta[i] = at
            return at + (spans[0, i] > 0).astype(jnp.int32)

        lax.fori_loop(root, blocks, place, jnp.int32(0))

        def moves(act):
            k = 0
            for ref in piece_refs:
                for j in range(ref.shape[0]):
                    for t in range(ref.shape[2] // BLOCK):
                        owner = owner_of(me[0], spots[k])
                        k += 1

                        @pl.when(spans[0, owner] > 0)
                        def _(owner=owner, ref=ref, j=j, t=t):
                            lane = pl.multiple_of(meta[owner] * BLOCK, BLOCK)
                            act(
                                pltpu.make_async_copy(
                                    ref.at[j, :, pl.ds(t * BLOCK, BLOCK)],
                                    raw.at[:, pl.ds(lane, BLOCK)],
                                    sem,
                                )
                            )

        moves(lambda copy: copy.start())
        moves(lambda copy: copy.wait())
        spot = lax.broadcasted_iota(jnp.int32, (depth, BLOCK), 1)

        def pack(i, total):
            @pl.when(spans[0, i] > 0)
            def _():
                offset = total & (BLOCK - 1)
                turn = (total + BLOCK - spans[1, i]) & (BLOCK - 1)
                block = raw[:, pl.ds(pl.multiple_of(meta[i] * BLOCK, BLOCK), BLOCK)]
                block = pltpu.roll(block.astype(jnp.float32), turn, 1)
                lane = pl.multiple_of(total - offset, BLOCK)
                here = keys[:, pl.ds(lane, BLOCK)].astype(jnp.float32)
                here = jnp.where(spot >= offset, block, here)
                keys[:, pl.ds(lane, BLOCK)] = here.astype(jnp.bfloat16)
                keys[:, pl.ds(lane + BLOCK, BLOCK)] = block.astype(jnp.bfloat16)

            return total + spans[0, i]

        total = lax.fori_loop(root, blocks, pack, jnp.int32(0))
        meta[blocks] = total
        lane = pl.multiple_of((total + BLOCK - 1) & -BLOCK, BLOCK)
        keys[:, pl.ds(lane, BLOCK)] = jnp.zeros((depth, BLOCK), jnp.bfloat16)

    seen = meta[blocks]
    used = lax.div(seen + (BLOCK - 1), jnp.int32(BLOCK))
    per = sub // s
    subs = group // per

    def chunk(lane, size, m_old=m_ref, l_old=l_ref, acc_old=acc_ref):
        lane = pl.multiple_of(lane, BLOCK)
        index = lane + lax.broadcasted_iota(jnp.int32, (1, size), 1)
        hide = jnp.where(index < seen, 0.0, HIDDEN)

        def score(k):
            q = q_ref[k * per : (k + 1) * per].reshape(sub, depth)
            return jnp.dot(q, keys[:, pl.ds(lane, size)], preferred_element_type=jnp.float32)

        def absorb(k, raw):
            r = pl.ds(k * sub, sub)
            sc = raw + hide
            old = m_old[r, :]
            m = jnp.maximum(old, jnp.max(sc, axis=1, keepdims=True))
            fade = jnp.exp2((old - m) * factor)
            p = jnp.exp2((sc - jnp.tile(m, (1, size // 128))) * factor)
            m_ref[r, :] = m
            l_ref[r, :] = l_old[r, :] * fade + lane_sums(p)
            acc_ref[r, :] = acc_old[r, :] * jnp.tile(fade, (1, lat // 128)) + lax.dot_general(
                p.astype(jnp.bfloat16),
                keys[:lat, pl.ds(lane, size)],
                NT,
                preferred_element_type=jnp.float32,
            )

        staged(subs, score, absorb)

    many = lax.div(used + 1, jnp.int32(wide))

    @pl.when(many > 0)
    def _():
        chunk(0, wide * BLOCK, m_in, l_in, acc_in)

    @pl.when(many == 0)
    def _():
        m_ref[...] = m_in[...]
        l_ref[...] = l_in[...]
        acc_ref[...] = acc_in[...]

    def big(i, carry):
        chunk(i * (wide * BLOCK), wide * BLOCK)
        return carry

    lax.fori_loop(1, many, big, 0)
    at = many * (wide * BLOCK)
    rem = used - many * wide
    size = wide // 2
    while size > 1:
        fits = rem + 1 >= size if size > 2 else rem > 0

        @pl.when(fits)
        def _(at=at, size=size):
            chunk(at, size * BLOCK)

        at = at + jnp.where(fits, size * BLOCK, 0)
        rem = rem - jnp.where(fits, size, 0)
        size //= 2

    for g in range(group):
        r = pl.ds(g * s, s)
        total = jnp.sum(l_ref[r, :], axis=1, keepdims=True)
        o = (acc_ref[r, :] * (1.0 / total)).astype(jnp.bfloat16)
        out_ref[:, g * vd : (g + 1) * vd] = jnp.dot(
            o, wuv_ref[g], preferred_element_type=jnp.float32
        ).astype(jnp.bfloat16)


def attend_rest(spans, me, spots, query, state, w_uv, pieces, scale, group=8, sub=1024, wide=8):
    heads, s, depth = query.shape
    lat, vd = w_uv.shape[1:]
    trunk = spans.shape[1] * BLOCK
    group = min(group, heads)
    sub = min(sub, group * s)
    total = group * s
    return pl.pallas_call(
        functools.partial(
            rest_kernel, pieces=len(pieces), spots=spots, sub=sub, wide=wide, scale=scale
        ),
        grid_spec=pltpu.PrefetchScalarGridSpec(
            num_scalar_prefetch=2,
            grid=(heads // group,),
            in_specs=[
                pl.BlockSpec((group, s, depth), lambda i, *_: (i, 0, 0)),
                pl.BlockSpec((total, lat), lambda i, *_: (i, 0)),
                pl.BlockSpec((total, 128), lambda i, *_: (i, 0)),
                pl.BlockSpec((total, 128), lambda i, *_: (i, 0)),
                pl.BlockSpec((group, lat, vd), lambda i, *_: (i, 0, 0)),
            ]
            + [pl.BlockSpec(memory_space=pl.ANY)] * len(pieces),
            out_specs=pl.BlockSpec((s, group * vd), lambda i, *_: (0, i)),
            scratch_shapes=[
                pltpu.VMEM((depth, trunk), jnp.bfloat16),
                pltpu.VMEM((depth, trunk), jnp.bfloat16),
                pltpu.VMEM((total, 128), jnp.float32),
                pltpu.VMEM((total, 128), jnp.float32),
                pltpu.VMEM((total, lat), jnp.float32),
                pltpu.SMEM((trunk // BLOCK + 1,), jnp.int32),
                pltpu.SemaphoreType.DMA,
            ],
        ),
        out_shape=jax.ShapeDtypeStruct((s, heads * vd), jnp.bfloat16),
        compiler_params=pltpu.CompilerParams(vmem_limit_bytes=60 << 20),
        cost_estimate=pl.CostEstimate(
            flops=heads * s * (trunk // 2) * (depth + lat),
            bytes_accessed=2 * (query.size + w_uv.size) + 4 * heads * s * (lat + 256),
            transcendentals=heads * s * trunk // 4,
        ),
        name="attend_rest",
    )(spans, me, *map(in_hbm, (query, *state, w_uv, *pieces)))


def swap(x, mask, devices):
    return lax.ppermute(x, AXES, [(i, i ^ mask) for i in range(devices)])


def gather_rows(rows, branches, heads):
    devices = branches * heads
    if rows.shape[0] % 16 or heads & (heads - 1):
        return [lax.all_gather(rows, "head", axis=0, tiled=True)], [(0, None, 1)]
    pieces = [rows] + [swap(rows, k, devices) for k in range(1, heads)]
    return pieces, [(0, k, heads) for k in range(heads)]


def is_cube(trunk, branches, heads):
    return trunk.shape[0] == BLOCK and branches == 8 and heads == 4


def gather_columns(trunk, branches, heads):
    devices = branches * heads
    plane = devices // 4
    mine = trunk.T[None]
    column = [mine] + [swap(mine, plane * d, devices) for d in (1, 2, 3)]
    layer = (lax.axis_index("branch") * heads + lax.axis_index("head")) // plane
    level = jnp.concatenate(column, axis=0)
    return jnp.concatenate(
        [lax.dynamic_slice_in_dim(level, layer ^ k, 1, 0) for k in range(4)], axis=0
    )


def block_spans(visible):
    marks = visible.reshape(-1, BLOCK)
    spot = jnp.arange(BLOCK, dtype=jnp.int32)[None, :]
    first = jnp.min(jnp.where(marks > 0, spot, BLOCK), axis=1)
    return jnp.stack([jnp.sum(marks, axis=1), first])


def make_shards(branches, heads):
    devices = branches * heads
    plane = devices // 4

    def shards(q_latent, seg_latent, trunk_latent, visible, w_uq, w_uk, w_uv):
        heads_here, nope, lat = w_uk.shape
        rope = w_uq.shape[1] // heads_here - nope
        scale = 1.0 / (nope + rope) ** 0.5
        cube = is_cube(trunk_latent, branches, heads)
        place = (lax.axis_index("branch") * heads + lax.axis_index("head")).astype(jnp.int32)
        me = place.reshape(1)
        rows, row_spots = gather_rows(q_latent, branches, heads)
        part = heads_here // 2
        project = functools.partial(make_query, me, rows, row_spots, visible, w_uq, w_uk)
        if cube:
            levels = gather_columns(trunk_latent, branches, heads)
            query = project(0, part)
            query, marks = lax.optimization_barrier((query, visible))
            spans = block_spans(marks)
            query, levels, seg_latent, spans = lax.optimization_barrier(
                (query, levels, seg_latent, spans)
            )
            root, others = levels[:1], levels[1:]
            around = (0, 2, 4, 6)
            root_here = [root] + [swap(root, k, devices) for k in around[1:]]
            query = project(part, heads_here - part, query)
            own, own_spots = gather_rows(seg_latent, branches, heads)
            query, root_here, others, own = lax.optimization_barrier(
                (query, root_here, others, own)
            )
            root_here = jnp.concatenate(root_here, axis=0)
            pieces = [root_here, swap(root_here, 1, devices)]
            masks = list(around) + [1 ^ k for k in around]
            root_spots = [(0, k, plane) for k in masks]
            rest = [others] + [swap(others, k, devices) for k in around[1:]]
            rest_spots = [(plane * d, k, plane) for k in masks for d in (1, 2, 3)]
        else:
            query = project(0, heads_here)
            spans = block_spans(visible)
            own, own_spots = gather_rows(seg_latent, branches, heads)
            whole = lax.all_gather(trunk_latent, AXES, axis=0, tiled=True).T[None]
            size = whole.shape[2] // 4
            pieces, rest = [whole[:, :, :size]], [whole[:, :, size:]]
            spots = [(k, None, 1) for k in range(whole.shape[2] // BLOCK)]
            root_spots, rest_spots = spots[: size // BLOCK], spots[size // BLOCK :]
        state = attend_root(
            me, own_spots, root_spots, query, own, pieces, visible.shape[1] // 4, lat, scale
        )
        state, rest = lax.optimization_barrier((state, rest))
        if cube:
            rest = rest + [swap(x, 1, devices) for x in rest]
        return attend_rest(spans, me, rest_spots, query, state, w_uv, rest, scale)

    return shards


def solution(mesh):
    placed = (
        P(("branch", "head"), None),
        P(("branch", "head"), None),
        P(("branch", "head"), None),
        P("branch", None),
        P(None, "head"),
        P("head", None, None),
        P("head", None, None),
    )
    return jax.shard_map(
        make_shards(mesh.shape["branch"], mesh.shape["head"]),
        mesh=mesh,
        in_specs=placed,
        out_specs=P("branch", "head"),
        check_vma=False,
    )
```

```python
import functools

import jax
import jax.numpy as jnp
import numpy as np
from jax import lax
from jax.experimental import pallas as pl
from jax.experimental.pallas import tpu as pltpu
from jax.sharding import PartitionSpec as P

AXES = ("branch", "head")
BLOCK = 128
HIDDEN = -1e30
LOG2E = 1.4426950408889634
NT = (((1,), (1,)), ((), ()))


def staged(count, score, absorb):
    ahead = score(0)
    for k in range(count):
        now = ahead
        if k + 1 < count:
            ahead = score(k + 1)
        absorb(k, now)


def in_hbm(x):
    return pltpu.with_memory_space_constraint(x, pltpu.HBM)


def owner_of(me, spot):
    offset, mask, plane = spot
    if mask is None:
        return jnp.int32(offset)
    return offset + (lax.rem(me, jnp.int32(plane)) ^ mask)


def query_kernel(me, *refs, pieces, spots, aliased):
    piece_refs = refs[:pieces]
    seen_ref, freq_ref, wuq_ref, wuk_ref = refs[pieces : pieces + 4]
    out_ref, qs, cos_ref, sin_ref = refs[pieces + 4 + aliased :]
    group, nope, lat = wuk_ref.shape
    rope = freq_ref.shape[1]
    width = nope + rope
    half = rope // 2

    @pl.when(pl.program_id(0) == 0)
    def _():
        for ref, spot in zip(piece_refs, spots):
            n = ref.shape[0]
            at = owner_of(me[0], spot)
            qs[pl.ds(pl.multiple_of(at * n, n), n), :] = ref[...]
        depth = jnp.sum(seen_ref[...].astype(jnp.float32), axis=1, keepdims=True)
        token = lax.broadcasted_iota(jnp.int32, cos_ref.shape, 0).astype(jnp.float32)
        angle = (token + depth) * freq_ref[...]
        side = lax.broadcasted_iota(jnp.int32, cos_ref.shape, 1)
        sine = jnp.sin(angle)
        cos_ref[...] = jnp.cos(angle)
        sin_ref[...] = jnp.where(side < half, -sine, sine)

    def project(k):
        return jnp.dot(
            qs[...],
            wuq_ref[:, 2 * k * width : 2 * (k + 1) * width],
            preferred_element_type=jnp.float32,
        )

    def absorb(k, q):
        for j in range(2):
            g = 2 * k + j
            q_nope = q[:, j * width : j * width + nope].astype(jnp.bfloat16)
            x = q[:, j * width + nope : (j + 1) * width]
            swapped = jnp.concatenate([x[:, half:], x[:, :half]], axis=1)
            q_rope = x * cos_ref[...] + swapped * sin_ref[...]
            q_abs = jnp.dot(q_nope, wuk_ref[g], preferred_element_type=jnp.float32)
            out_ref[g, :, :lat] = q_abs.astype(jnp.bfloat16)
            out_ref[g, :, lat:] = q_rope.astype(jnp.bfloat16)

    staged(group // 2, project, absorb)


def make_query(me, pieces, spots, seen, w_uq, w_uk, start, count, before=None, group=8):
    seg_len = pieces[0].shape[0] * len(pieces)
    rank = w_uq.shape[0]
    heads, nope, lat = w_uk.shape
    width = w_uq.shape[1] // heads
    rope = width - nope
    group = min(group, count)
    base = start // group
    powers = 10000.0 ** (-2.0 * np.arange(rope // 2) / rope)
    freq = np.concatenate([powers, powers])[None].astype(np.float32)
    aliased = 0 if before is None else 1
    return pl.pallas_call(
        functools.partial(query_kernel, pieces=len(pieces), spots=spots, aliased=aliased),
        grid_spec=pltpu.PrefetchScalarGridSpec(
            num_scalar_prefetch=1,
            grid=(count // group,),
            in_specs=[pl.BlockSpec((p.shape[0], rank), lambda i, *_: (0, 0)) for p in pieces]
            + [
                pl.BlockSpec(seen.shape, lambda i, *_: (0, 0)),
                pl.BlockSpec(freq.shape, lambda i, *_: (0, 0)),
                pl.BlockSpec((rank, group * width), lambda i, *_: (0, base + i)),
                pl.BlockSpec((group, nope, lat), lambda i, *_: (base + i, 0, 0)),
            ]
            + [pl.BlockSpec(memory_space=pl.ANY)] * aliased,
            out_specs=pl.BlockSpec((group, seg_len, lat + rope), lambda i, *_: (base + i, 0, 0)),
            scratch_shapes=[
                pltpu.VMEM((seg_len, rank), jnp.bfloat16),
                pltpu.VMEM((seg_len, rope), jnp.float32),
                pltpu.VMEM((seg_len, rope), jnp.float32),
            ],
        ),
        out_shape=jax.ShapeDtypeStruct((heads, seg_len, lat + rope), jnp.bfloat16),
        input_output_aliases={len(pieces) + 5: 0} if aliased else {},
        compiler_params=pltpu.CompilerParams(vmem_limit_bytes=60 << 20),
        cost_estimate=pl.CostEstimate(
            flops=2 * seg_len * count * (rank * width + nope * lat),
            bytes_accessed=2 * count * (rank * width + nope * lat + seg_len * (lat + rope)),
            transcendentals=0,
        ),
        name="query",
    )(me, *pieces, seen, freq, w_uq, w_uk, *([before] if aliased else []))


def lane_sums(p):
    return functools.reduce(
        jnp.add, [p[:, j : j + 128] for j in range(0, p.shape[1], 128)]
    )


def root_kernel(
    me, q_ref, *rest, rows_n, pieces, row_spots, spots, sub, scale, lat
):
    row_refs, piece_refs = rest[:rows_n], rest[rows_n : rows_n + pieces]
    acc_ref, m_ref, l_ref, keys, own, sem = rest[rows_n + pieces :]
    s, depth = own.shape
    first = keys.shape[1]
    factor = scale * LOG2E

    @pl.when(pl.program_id(0) == 0)
    def _():
        copies = []
        for ref in piece_refs:
            for j in range(ref.shape[0]):
                for t in range(ref.shape[2] // BLOCK):
                    lane = pl.multiple_of((1 + owner_of(me[0], spots[len(copies)])) * BLOCK, BLOCK)
                    copies.append(
                        pltpu.make_async_copy(
                            ref.at[j, :, pl.ds(t * BLOCK, BLOCK)],
                            keys.at[:, pl.ds(lane, BLOCK)],
                            sem,
                        )
                    )
        for copy in copies:
            copy.start()
        for k, ref in enumerate(row_refs):
            n = ref.shape[0]
            at = owner_of(me[0], row_spots[k])
            own[pl.ds(pl.multiple_of(at * n, n), n), :] = ref[...]
        keys[:, :s] = own[...].T
        for copy in copies:
            copy.wait()

    per = sub // s
    row = lax.broadcasted_iota(jnp.int32, (s, s), 0)
    col = lax.broadcasted_iota(jnp.int32, (s, s), 1)
    causal = jnp.where(col <= row, 0.0, HIDDEN)

    def score(k):
        q = q_ref[k * per : (k + 1) * per].reshape(sub, depth)
        return jnp.dot(q, keys[...], preferred_element_type=jnp.float32)

    def absorb(k, raw):
        r = pl.ds(k * sub, sub)
        head = (raw[:, :s].reshape(per, s, s) + causal[None]).reshape(sub, s)
        sc = jnp.concatenate([head, raw[:, s:]], axis=1)
        m = jnp.max(sc, axis=1, keepdims=True)
        p = jnp.exp2((sc - m) * factor)
        m_ref[r, :] = jnp.broadcast_to(m, (sub, 128))
        l_ref[r, :] = lane_sums(p)
        acc_ref[r, :] = lax.dot_general(
            p.astype(jnp.bfloat16), keys[:lat, :], NT, preferred_element_type=jnp.float32
        )

    staged(q_ref.shape[0] // per, score, absorb)


def attend_root(me, row_spots, spots, query, row_pieces, pieces, root, lat, scale, group=8, sub=512):
    heads, s, depth = query.shape
    group = min(group, heads)
    sub = min(sub, group * s)
    total = group * s
    width = row_pieces[0].shape[1]
    out = lambda n: jax.ShapeDtypeStruct((heads * s, n), jnp.float32)
    return pl.pallas_call(
        functools.partial(
            root_kernel,
            rows_n=len(row_pieces),
            pieces=len(pieces),
            row_spots=row_spots,
            spots=spots,
            sub=sub,
            scale=scale,
            lat=lat,
        ),
        grid_spec=pltpu.PrefetchScalarGridSpec(
            num_scalar_prefetch=1,
            grid=(heads // group,),
            in_specs=[pl.BlockSpec((group, s, depth), lambda i, *_: (i, 0, 0))]
            + [pl.BlockSpec((p.shape[0], width), lambda i, *_: (0, 0)) for p in row_pieces]
            + [pl.BlockSpec(memory_space=pl.ANY)] * len(pieces),
            out_specs=[
                pl.BlockSpec((total, lat), lambda i, *_: (i, 0)),
                pl.BlockSpec((total, 128), lambda i, *_: (i, 0)),
                pl.BlockSpec((total, 128), lambda i, *_: (i, 0)),
            ],
            scratch_shapes=[
                pltpu.VMEM((depth, s + root), jnp.bfloat16),
                pltpu.VMEM((s, depth), jnp.bfloat16),
                pltpu.SemaphoreType.DMA,
            ],
        ),
        out_shape=[out(lat), out(128), out(128)],
        compiler_params=pltpu.CompilerParams(vmem_limit_bytes=60 << 20),
        cost_estimate=pl.CostEstimate(
            flops=4 * heads * s * (s + root) * (depth + lat),
            bytes_accessed=2 * query.size + 4 * heads * s * (lat + 256),
            transcendentals=heads * s * (s + root),
        ),
        name="attend_root",
    )(me, in_hbm(query), *map(in_hbm, row_pieces), *map(in_hbm, pieces))


def rest_kernel(
    spans, me, q_ref, acc_in, m_in, l_in, wuv_ref, *rest, pieces, spots, sub, wide, scale
):
    piece_refs, out_ref = rest[:pieces], rest[pieces]
    raw, keys, m_ref, l_ref, acc_ref, meta, sem = rest[pieces + 1 :]
    group, lat, vd = wuv_ref.shape
    s, depth = q_ref.shape[1:]
    blocks = spans.shape[1]
    root = blocks // 4
    factor = scale * LOG2E

    @pl.when(pl.program_id(0) == 0)
    def _():
        def place(i, at):
            meta[i] = at
            return at + (spans[0, i] > 0).astype(jnp.int32)

        lax.fori_loop(root, blocks, place, jnp.int32(0))

        def moves(act):
            k = 0
            for ref in piece_refs:
                for j in range(ref.shape[0]):
                    for t in range(ref.shape[2] // BLOCK):
                        owner = owner_of(me[0], spots[k])
                        k += 1

                        @pl.when(spans[0, owner] > 0)
                        def _(owner=owner, ref=ref, j=j, t=t):
                            lane = pl.multiple_of(meta[owner] * BLOCK, BLOCK)
                            act(
                                pltpu.make_async_copy(
                                    ref.at[j, :, pl.ds(t * BLOCK, BLOCK)],
                                    raw.at[:, pl.ds(lane, BLOCK)],
                                    sem,
                                )
                            )

        moves(lambda copy: copy.start())
        moves(lambda copy: copy.wait())
        spot = lax.broadcasted_iota(jnp.int32, (depth, BLOCK), 1)

        def pack(i, total):
            @pl.when(spans[0, i] > 0)
            def _():
                offset = total & (BLOCK - 1)
                turn = (total + BLOCK - spans[1, i]) & (BLOCK - 1)
                block = raw[:, pl.ds(pl.multiple_of(meta[i] * BLOCK, BLOCK), BLOCK)]
                block = pltpu.roll(block.astype(jnp.float32), turn, 1)
                lane = pl.multiple_of(total - offset, BLOCK)
                here = keys[:, pl.ds(lane, BLOCK)].astype(jnp.float32)
                here = jnp.where(spot >= offset, block, here)
                keys[:, pl.ds(lane, BLOCK)] = here.astype(jnp.bfloat16)
                keys[:, pl.ds(lane + BLOCK, BLOCK)] = block.astype(jnp.bfloat16)

            return total + spans[0, i]

        total = lax.fori_loop(root, blocks, pack, jnp.int32(0))
        meta[blocks] = total
        lane = pl.multiple_of((total + BLOCK - 1) & -BLOCK, BLOCK)
        keys[:, pl.ds(lane, BLOCK)] = jnp.zeros((depth, BLOCK), jnp.bfloat16)

    seen = meta[blocks]
    used = lax.div(seen + (BLOCK - 1), jnp.int32(BLOCK))
    per = sub // s
    subs = group // per

    def chunk(lane, size, m_old=m_ref, l_old=l_ref, acc_old=acc_ref):
        lane = pl.multiple_of(lane, BLOCK)
        index = lane + lax.broadcasted_iota(jnp.int32, (1, size), 1)
        hide = jnp.where(index < seen, 0.0, HIDDEN)

        def score(k):
            q = q_ref[k * per : (k + 1) * per].reshape(sub, depth)
            return jnp.dot(q, keys[:, pl.ds(lane, size)], preferred_element_type=jnp.float32)

        def absorb(k, raw):
            r = pl.ds(k * sub, sub)
            sc = raw + hide
            old = m_old[r, :]
            m = jnp.maximum(old, jnp.max(sc, axis=1, keepdims=True))
            fade = jnp.exp2((old - m) * factor)
            p = jnp.exp2((sc - jnp.tile(m, (1, size // 128))) * factor)
            m_ref[r, :] = m
            l_ref[r, :] = l_old[r, :] * fade + lane_sums(p)
            acc_ref[r, :] = acc_old[r, :] * jnp.tile(fade, (1, lat // 128)) + lax.dot_general(
                p.astype(jnp.bfloat16),
                keys[:lat, pl.ds(lane, size)],
                NT,
                preferred_element_type=jnp.float32,
            )

        staged(subs, score, absorb)

    many = lax.div(used + 1, jnp.int32(wide))

    @pl.when(many > 0)
    def _():
        chunk(0, wide * BLOCK, m_in, l_in, acc_in)

    @pl.when(many == 0)
    def _():
        m_ref[...] = m_in[...]
        l_ref[...] = l_in[...]
        acc_ref[...] = acc_in[...]

    def big(i, carry):
        chunk(i * (wide * BLOCK), wide * BLOCK)
        return carry

    lax.fori_loop(1, many, big, 0)
    at = many * (wide * BLOCK)
    rem = used - many * wide
    size = wide // 2
    while size > 1:
        fits = rem + 1 >= size if size > 2 else rem > 0

        @pl.when(fits)
        def _(at=at, size=size):
            chunk(at, size * BLOCK)

        at = at + jnp.where(fits, size * BLOCK, 0)
        rem = rem - jnp.where(fits, size, 0)
        size //= 2

    for g in range(group):
        r = pl.ds(g * s, s)
        total = jnp.sum(l_ref[r, :], axis=1, keepdims=True)
        o = (acc_ref[r, :] * (1.0 / total)).astype(jnp.bfloat16)
        out_ref[:, g * vd : (g + 1) * vd] = jnp.dot(
            o, wuv_ref[g], preferred_element_type=jnp.float32
        ).astype(jnp.bfloat16)


def attend_rest(spans, me, spots, query, state, w_uv, pieces, scale, group=8, sub=1024, wide=8):
    heads, s, depth = query.shape
    lat, vd = w_uv.shape[1:]
    trunk = spans.shape[1] * BLOCK
    group = min(group, heads)
    sub = min(sub, group * s)
    total = group * s
    return pl.pallas_call(
        functools.partial(
            rest_kernel, pieces=len(pieces), spots=spots, sub=sub, wide=wide, scale=scale
        ),
        grid_spec=pltpu.PrefetchScalarGridSpec(
            num_scalar_prefetch=2,
            grid=(heads // group,),
            in_specs=[
                pl.BlockSpec((group, s, depth), lambda i, *_: (i, 0, 0)),
                pl.BlockSpec((total, lat), lambda i, *_: (i, 0)),
                pl.BlockSpec((total, 128), lambda i, *_: (i, 0)),
                pl.BlockSpec((total, 128), lambda i, *_: (i, 0)),
                pl.BlockSpec((group, lat, vd), lambda i, *_: (i, 0, 0)),
            ]
            + [pl.BlockSpec(memory_space=pl.ANY)] * len(pieces),
            out_specs=pl.BlockSpec((s, group * vd), lambda i, *_: (0, i)),
            scratch_shapes=[
                pltpu.VMEM((depth, trunk), jnp.bfloat16),
                pltpu.VMEM((depth, trunk), jnp.bfloat16),
                pltpu.VMEM((total, 128), jnp.float32),
                pltpu.VMEM((total, 128), jnp.float32),
                pltpu.VMEM((total, lat), jnp.float32),
                pltpu.SMEM((trunk // BLOCK + 1,), jnp.int32),
                pltpu.SemaphoreType.DMA,
            ],
        ),
        out_shape=jax.ShapeDtypeStruct((s, heads * vd), jnp.bfloat16),
        compiler_params=pltpu.CompilerParams(vmem_limit_bytes=60 << 20),
        cost_estimate=pl.CostEstimate(
            flops=heads * s * (trunk // 2) * (depth + lat),
            bytes_accessed=2 * (query.size + w_uv.size) + 4 * heads * s * (lat + 256),
            transcendentals=heads * s * trunk // 4,
        ),
        name="attend_rest",
    )(spans, me, *map(in_hbm, (query, *state, w_uv, *pieces)))


def swap(x, mask, devices):
    return lax.ppermute(x, AXES, [(i, i ^ mask) for i in range(devices)])


def gather_rows(rows, branches, heads):
    devices = branches * heads
    if rows.shape[0] % 16 or heads & (heads - 1):
        return [lax.all_gather(rows, "head", axis=0, tiled=True)], [(0, None, 1)]
    pieces = [rows] + [swap(rows, k, devices) for k in range(1, heads)]
    return pieces, [(0, k, heads) for k in range(heads)]


def is_cube(trunk, branches, heads):
    return trunk.shape[0] == BLOCK and branches == 8 and heads == 4


def gather_columns(trunk, branches, heads):
    devices = branches * heads
    plane = devices // 4
    mine = trunk.T[None]
    column = [mine] + [swap(mine, plane * d, devices) for d in (1, 2, 3)]
    layer = (lax.axis_index("branch") * heads + lax.axis_index("head")) // plane
    level = jnp.concatenate(column, axis=0)
    return jnp.concatenate(
        [lax.dynamic_slice_in_dim(level, layer ^ k, 1, 0) for k in range(4)], axis=0
    )


def block_spans(visible):
    marks = visible.reshape(-1, BLOCK)
    spot = jnp.arange(BLOCK, dtype=jnp.int32)[None, :]
    first = jnp.min(jnp.where(marks > 0, spot, BLOCK), axis=1)
    return jnp.stack([jnp.sum(marks, axis=1), first])


def make_shards(branches, heads):
    devices = branches * heads
    plane = devices // 4

    def shards(q_latent, seg_latent, trunk_latent, visible, w_uq, w_uk, w_uv):
        heads_here, nope, lat = w_uk.shape
        rope = w_uq.shape[1] // heads_here - nope
        scale = 1.0 / (nope + rope) ** 0.5
        cube = is_cube(trunk_latent, branches, heads)
        place = (lax.axis_index("branch") * heads + lax.axis_index("head")).astype(jnp.int32)
        me = place.reshape(1)
        rows, row_spots = gather_rows(q_latent, branches, heads)
        part = heads_here // 2
        project = functools.partial(make_query, me, rows, row_spots, visible, w_uq, w_uk)
        if cube:
            levels = gather_columns(trunk_latent, branches, heads)
            query = project(0, part)
            query, marks = lax.optimization_barrier((query, visible))
            spans = block_spans(marks)
            query, levels, seg_latent, spans = lax.optimization_barrier(
                (query, levels, seg_latent, spans)
            )
            root, others = levels[:1], levels[1:]
            around = (0, 2, 4, 6)
            root_here = [root] + [swap(root, k, devices) for k in around[1:]]
            query = project(part, heads_here - part, query)
            own, own_spots = gather_rows(seg_latent, branches, heads)
            query, root_here, others, own = lax.optimization_barrier(
                (query, root_here, others, own)
            )
            root_here = jnp.concatenate(root_here, axis=0)
            pieces = [root_here, swap(root_here, 1, devices)]
            masks = list(around) + [1 ^ k for k in around]
            root_spots = [(0, k, plane) for k in masks]
            rest = [others] + [swap(others, k, devices) for k in around[1:]]
            rest_spots = [(plane * d, k, plane) for k in masks for d in (1, 2, 3)]
        else:
            query = project(0, heads_here)
            spans = block_spans(visible)
            own, own_spots = gather_rows(seg_latent, branches, heads)
            whole = lax.all_gather(trunk_latent, AXES, axis=0, tiled=True).T[None]
            size = whole.shape[2] // 4
            pieces, rest = [whole[:, :, :size]], [whole[:, :, size:]]
            spots = [(k, None, 1) for k in range(whole.shape[2] // BLOCK)]
            root_spots, rest_spots = spots[: size // BLOCK], spots[size // BLOCK :]
        state = attend_root(
            me, own_spots, root_spots, query, own, pieces, visible.shape[1] // 4, lat, scale
        )
        early = [swap(others, 1, devices)] if cube else []
        state, rest, early = lax.optimization_barrier((state, rest, early))
        if cube:
            rest = rest + early + [swap(x, 1, devices) for x in rest[1:]]
        return attend_rest(spans, me, rest_spots, query, state, w_uv, rest, scale)

    return shards


def solution(mesh):
    placed = (
        P(("branch", "head"), None),
        P(("branch", "head"), None),
        P(("branch", "head"), None),
        P("branch", None),
        P(None, "head"),
        P("head", None, None),
        P("head", None, None),
    )
    return jax.shard_map(
        make_shards(mesh.shape["branch"], mesh.shape["head"]),
        mesh=mesh,
        in_specs=placed,
        out_specs=P("branch", "head"),
        check_vma=False,
    )
```
